32 devices in a mesh: pipe: 2 (over y), wide: 8 (over z, x), tp: 2 (over core).
Axes of the slice: x: 2, y: 2, z: 4, core: 2. Of those that a mesh axis runs over, the one named last changes fastest.
Arguments:
- block_input: bfloat16 [2, 2, 1024, 768], P(None, None, ('wide', 'tp')), may hold values from -6 to 6
- out_cotangent: bfloat16 [2, 2, 1024, 768], P(None, None, ('wide', 'tp')), may hold values from -6 to 6
- routes: int32 [2, 2, 2, 1024, 1], P('pipe', None, None, 'wide'), may hold values from 0 to 7; in each aligned block of 64 rows (0 to 63, 64 to 127, ..., all dimensions but the last counted through in order) at most 12 rows name the same one
- attn_gain: bfloat16 [2, 768], P('pipe', ('wide', 'tp')), may hold values from 0.5 to 1.5
- query_weight: bfloat16 [2, 768, 768], P('pipe', 'wide', 'tp'), may hold values from -0.21875 to 0.21875
- key_weight: bfloat16 [2, 768, 768], P('pipe', 'wide', 'tp'), may hold values from -0.21875 to 0.21875
- value_weight: bfloat16 [2, 768, 768], P('pipe', 'wide', 'tp'), may hold values from -0.21875 to 0.21875
- output_weight: bfloat16 [2, 768, 768], P('pipe', 'tp', 'wide'), may hold values from -0.4375 to 0.4375
- moe_gain: bfloat16 [2, 768], P('pipe', ('wide', 'tp')), may hold values from 0.5 to 1.5
- router_weight: bfloat16 [2, 768, 8], P('pipe', ('wide', 'tp')), may hold values from -0.15625 to 0.15625
- expert_in: bfloat16 [2, 8, 768, 3072], P('pipe', 'wide', None, 'tp'), may hold values from -0.21875 to 0.21875
- expert_out: bfloat16 [2, 8, 3072, 768], P('pipe', 'wide', 'tp'), may hold values from -0.3125 to 0.3125
Outputs:
- layer_outputs: bfloat16 [2, 2, 2, 1024, 768], P('pipe', None, None, ('wide', 'tp'))
- input_grads: bfloat16 [2, 2, 2, 1024, 768], P('pipe', None, None, ('wide', 'tp'))
- attn_gain_grad: float32 [2, 768], P('pipe', ('wide', 'tp'))
- query_grad: float32 [2, 768, 768], P('pipe', 'wide', 'tp')
- key_grad: float32 [2, 768, 768], P('pipe', 'wide', 'tp')
- value_grad: float32 [2, 768, 768], P('pipe', 'wide', 'tp')
- output_grad: float32 [2, 768, 768], P('pipe', 'tp', 'wide')
- moe_gain_grad: float32 [2, 768], P('pipe', ('wide', 'tp'))
- router_grad: float32 [2, 768, 8], P('pipe', ('wide', 'tp'))
- expert_in_grad: float32 [2, 8, 768, 3072], P('pipe', 'wide', None, 'tp')
- expert_out_grad: float32 [2, 8, 3072, 768], P('pipe', 'wide', 'tp')
The draws below stay inside these ranges and needn't reach their ends.
Inputs may be any that keep to these rules, and one draw needn't show every extreme that they name: `routes`: within each aligned block of 64 positions of one sequence (all leading dimensions taken in order), no expert is named more than 12 times, and some block names one expert exactly 12 times.
All inputs are finite; a program needn't handle non-finite values.
Results may differ from the reference program's by a relative error of at most 0.03.
Values may be sent and summed in bfloat16 or wider, within the bound.
No kernel may reach another device: no remote copies, remote signals or barrier semaphores. Data moves between devices by JAX's collectives and lax.ppermute only.
A program may use at most 192 MiB of HBM per device.

```python
import math
from functools import partial
import jax
import jax.numpy as jnp
import numpy as np
from jax import lax

D = 768
HEADS = 12
HEAD_DIM = 64
FF = 3072
MB = 2
SEQ_MB = 2
INNER = 768
EXPERTS = 8
LEN = 1024
HALF = 64
MOST = 12
N_TP = 2


def shard_levels(own_key, shape, pieces, least, top_value):
    gain, own = 1.0, jax.random.fold_in(own_key, 6)
    for axis_at, blocks in pieces:
        draws = jnp.exp(jax.random.uniform(jax.random.fold_in(own, axis_at), (blocks,), jnp.float32, least / len(pieces), top_value / len(pieces)))
        gain = gain * jnp.repeat(draws, shape[axis_at] // blocks).reshape([-1 if axis == axis_at else 1 for axis in range(len(shape))])
    return gain


def routed_block(own_key, own, number, rows, amount, top, reach, slope):
    sequence = jax.random.permutation(own_key, amount)
    packed, common = shares(amount, rows * top, reach, slope, True), shares(amount, rows * top, reach, slope, False)
    places = jnp.arange(amount)

    def named(sizes, offset_by):
        used = int((sizes > 0).sum())
        fixed = max(1, used // 4)
        passed = fixed + (places - fixed + offset_by * (used - fixed)) % max(1, amount - fixed)
        return jnp.zeros((amount,), jnp.int32).at[sequence[jnp.where(places < fixed, places, passed)]].set(jnp.asarray(sizes, jnp.int32))

    sizes = jnp.where(number % 4 == 0, named(packed, number // 4), named(common, number - number // 4 - 1))
    mixed = jax.random.permutation(jax.random.fold_in(own, 3), amount)
    donor, sink = mixed[0:amount // 2 * 2:2], mixed[1:amount // 2 * 2:2]
    room = jnp.minimum(sizes[donor] - 1, reach - sizes[sink]) // 2
    room = jnp.where((donor == sequence[0]) | (sink == sequence[0]) | (sizes[sink] == 0), 0, jnp.maximum(room, 0))
    passed = jax.random.randint(jax.random.fold_in(own, 4), (amount // 2,), 0, 1 << 20) % (room + 1)
    sizes = sizes.at[donor].add(-passed).at[sink].add(passed)
    items = jnp.searchsorted(jnp.cumsum(sizes), jnp.arange(rows * top), side="right").astype(jnp.int32)
    grid = items.reshape(top, rows).T
    grid = grid[jax.random.permutation(jax.random.fold_in(own, 1), rows)]
    offset_by = jax.random.randint(jax.random.fold_in(own, 2), (rows, 1), 0, top)
    return jnp.take_along_axis(grid, (jnp.arange(top)[None, :] + offset_by) % top, axis=1)


def shares(amount, total, limit, lean, full):
    loads = [(1 << 20) // math.isqrt(grade ** lean) + 1 for grade in range(1, amount + 1)]
    largest = limit if full else min(limit, max(-(-total // amount), total * loads[0] // sum(loads)))
    least = 1 if total - largest >= amount - 1 else 0
    given, surplus = [largest] + [least] * (amount - 1), total - largest - least * (amount - 1)
    while surplus > 0:
        free = [i for i in range(1, amount) if given[i] < largest] or [i for i in range(1, amount) if given[i] < limit]
        mass, remaining = sum([loads[i] for i in free]), surplus
        for i in free:
            extra = min(limit - given[i], max(1, remaining * loads[i] // mass), surplus)
            given[i] = given[i] + extra
            surplus = surplus - extra
    return np.array(given)


def noise(rng, dims, deviation, limit, split=(), kind=jnp.bfloat16):
    drawn = jax.random.normal(rng, dims, jnp.float32) * deviation
    if len(split) > 0:
        drawn = shard_levels(rng, dims, split, -0.22, 0.18) * drawn
    return jnp.clip(drawn, min=-limit, max=limit).astype(kind)


def setup_inputs(seed: int = 0) -> dict:
    key_list = jax.random.split(jax.random.key(seed), 13)
    block_input = noise(key_list[0], (MB, SEQ_MB, LEN, D), 1.0, 6.0, ((2, 16),))
    out_cotangent = noise(key_list[1], (MB, SEQ_MB, LEN, D), 1.0, 6.0, ((2, 16),))
    routes_keys = jax.random.split(jax.random.fold_in(key_list[2], 1), 2 * MB * SEQ_MB * LEN // HALF)
    routes_turns = jax.random.permutation(jax.random.fold_in(key_list[2], 3), 2 * MB * SEQ_MB * LEN // HALF)
    routes = jax.vmap(lambda own, number: routed_block(jax.random.fold_in(key_list[2], 2), own, number, HALF, EXPERTS, 1, MOST, 1))(routes_keys, routes_turns).reshape((2, MB, SEQ_MB, LEN, 1))
    attn_gain = jnp.clip(1.0 + 0.1 * jax.random.normal(key_list[3], (2, D), jnp.float32), 0.5, 1.5).astype(jnp.bfloat16)
    query_weight = noise(key_list[4], (2, D, INNER), D ** -0.5, 0.21875, ((0, 2), (1, 8), (2, 2)))
    key_weight = noise(key_list[5], (2, D, INNER), D ** -0.5, 0.21875, ((0, 2), (1, 8), (2, 2)))
    value_weight = noise(key_list[6], (2, D, INNER), D ** -0.5, 0.21875, ((0, 2), (1, 8), (2, 2)))
    output_weight = noise(key_list[7], (2, INNER, D), (INNER // 4) ** -0.5, 0.4375, ((0, 2), (1, 2), (2, 8)))
    moe_gain = jnp.clip(1.0 + 0.1 * jax.random.normal(key_list[8], (2, D), jnp.float32), 0.5, 1.5).astype(jnp.bfloat16)
    router_weight = noise(key_list[9], (2, D, EXPERTS), (2 * D) ** -0.5, 0.15625, ((0, 2), (1, 16)))
    expert_in = noise(key_list[10], (2, EXPERTS, D, FF), D ** -0.5, 0.21875, ((0, 2), (1, 8), (3, 2)))
    expert_out = noise(key_list[11], (2, EXPERTS, FF, D), (max(1, FF // EXPERTS)) ** -0.5, 0.3125, ((0, 2), (1, 8), (2, 2)))
    return {"block_input": block_input, "out_cotangent": out_cotangent, "routes": routes, "attn_gain": attn_gain, "query_weight": query_weight, "key_weight": key_weight, "value_weight": value_weight, "output_weight": output_weight, "moe_gain": moe_gain, "router_weight": router_weight, "expert_in": expert_in, "expert_out": expert_out}


EPSILON = 1e-06
SCORE_SCALE = 0.125
HIGHEST = lax.Precision.HIGHEST

@jax.custom_vjp
def low(v):
    return lax.optimization_barrier(v.astype(jnp.bfloat16)).astype(jnp.float32)

@jax.custom_vjp
def low_back(v):
    return v

def low_keep(v):
    return (low(v), None)

def low_pass(kept, grad):
    return (grad,)

def back_keep(v):
    return (v, None)

def back_low(kept, grad):
    return (low(grad),)
low.defvjp(low_keep, low_pass)
low_back.defvjp(back_keep, back_low)

def matmul_high(left, right):
    return jnp.dot(left, right, precision=HIGHEST, preferred_element_type=jnp.float32)

def rms_scaled(values, gain_vector):
    return values * lax.rsqrt(lax.optimization_barrier(jnp.mean(values * values, axis=-1, keepdims=True)) + EPSILON) * gain_vector

def attend_sequence(packed_triple):
    queries, keys, values = packed_triple
    block_len = min(512, LEN)

    def one_block(query_block):
        scores = low_back(SCORE_SCALE * jnp.einsum('qhe,khe->hqk', query_block, keys, precision=HIGHEST))
        weights = low(jax.nn.softmax(scores, axis=-1))
        return jnp.einsum('hqk,khe->qhe', weights, values, precision=HIGHEST)
    blocks = queries.reshape(LEN // block_len, block_len, HEADS, HEAD_DIM)
    return lax.map(jax.checkpoint(one_block), blocks).reshape(LEN, HEADS, HEAD_DIM)

def experts_apply(normed, route_ids, w_in, w_out):
    flat_rows = normed.reshape(-1, D)
    expert_ids = route_ids.reshape(-1).astype(jnp.int32)
    expert_hits = (expert_ids[:, None] == jnp.arange(EXPERTS, dtype=jnp.int32)[None, :]).astype(jnp.int32)
    slot_rank = lax.optimization_barrier(jnp.sum((jnp.cumsum(expert_hits, axis=0) - 1) * expert_hits, axis=1)).astype(jnp.int32)
    capacity = flat_rows.shape[0] // HALF * MOST
    part_width = FF // N_TP
    combined = jnp.zeros((flat_rows.shape[0], D), jnp.float32)
    for block_index in range(N_TP):
        lower = block_index * part_width
        rows_in = low_back(flat_rows)
        slots = jnp.zeros((EXPERTS, capacity, D), jnp.float32).at[expert_ids, slot_rank].set(rows_in)
        pre_act = low_back(jnp.einsum('esd,edf->esf', slots, w_in[:, :, lower:lower + part_width], precision=HIGHEST))
        activated = low(jax.nn.gelu(pre_act))
        result = low(low_back(jnp.einsum('esf,efd->esd', activated, w_out[:, lower:lower + part_width, :], precision=HIGHEST)))
        combined = combined + result[expert_ids, slot_rank]
    return combined.reshape(normed.shape)

def layer(route_ids, inputs, gain_a, w_query, w_key, w_value, w_output, gain_b, w_router, w_in, w_out):
    seq_count = inputs.shape[0]
    normed_a = low(rms_scaled(inputs, gain_a))
    queries = low(low_back(matmul_high(normed_a, w_query))).reshape(seq_count, LEN, HEADS, HEAD_DIM)
    keys = low(low_back(matmul_high(normed_a, w_key))).reshape(seq_count, LEN, HEADS, HEAD_DIM)
    values = low(low_back(matmul_high(normed_a, w_value))).reshape(seq_count, LEN, HEADS, HEAD_DIM)
    attended = lax.map(attend_sequence, (queries, keys, values)).reshape(seq_count, LEN, INNER)
    attended = low(low_back(attended))
    hidden = inputs + low_back(matmul_high(attended, w_output))
    normed_b = low(rms_scaled(hidden, gain_b))
    logits = matmul_high(normed_b, w_router)
    router_probs = jax.nn.softmax(logits, axis=-1)
    chosen = (route_ids[..., None] == jnp.arange(EXPERTS, dtype=jnp.int32)).astype(jnp.float32)
    gate = lax.optimization_barrier(jnp.sum(router_probs * chosen, axis=-1))
    mixed = experts_apply(normed_b, route_ids, w_in, w_out)
    return hidden + gate[..., None] * mixed

def reference(block_input, out_cotangent, routes, attn_gain, query_weight, key_weight, value_weight, output_weight, moe_gain, router_weight, expert_in, expert_out):
    weight_arrays = (attn_gain, query_weight, key_weight, value_weight, output_weight, moe_gain, router_weight, expert_in, expert_out)
    weight_sets = [tuple((array[section_index].astype(jnp.float32) for array in weight_arrays)) for section_index in range(2)]
    grad_totals = [[jnp.zeros_like(weight) for weight in weight_sets[section_index]] for section_index in range(2)]
    first_outputs, second_outputs, first_grads, second_grads = ([], [], [], [])
    for micro_step in range(MB):
        inputs = block_input[micro_step].astype(jnp.float32)
        first_out, first_vjp = jax.vjp(partial(layer, routes[0, micro_step, :, :, 0]), inputs, *weight_sets[0])
        first_low = first_out.astype(jnp.bfloat16)
        second_out, second_vjp = jax.vjp(partial(layer, routes[1, micro_step, :, :, 0]), first_low.astype(jnp.float32), *weight_sets[1])
        second_cot = second_vjp(out_cotangent[micro_step].astype(jnp.float32))
        passed_grad = second_cot[0].astype(jnp.bfloat16)
        first_cot = first_vjp(passed_grad.astype(jnp.float32))
        for slot_index in range(len(weight_arrays)):
            grad_totals[0][slot_index] = grad_totals[0][slot_index] + first_cot[slot_index + 1]
            grad_totals[1][slot_index] = grad_totals[1][slot_index] + second_cot[slot_index + 1]
        first_outputs.append(first_low)
        second_outputs.append(second_out.astype(jnp.bfloat16))
        first_grads.append(first_cot[0].astype(jnp.bfloat16))
        second_grads.append(passed_grad)
    layer_outputs = jnp.stack([jnp.stack(first_outputs), jnp.stack(second_outputs)])
    input_grads = jnp.stack([jnp.stack(first_grads), jnp.stack(second_grads)])
    stacked = [jnp.stack([grad_totals[0][slot_index], grad_totals[1][slot_index]]) for slot_index in range(len(weight_arrays))]
    return (layer_outputs, input_grads, stacked[0], stacked[1], stacked[2], stacked[3], stacked[4], stacked[5], stacked[6], stacked[7], stacked[8])
```

```python
import jax
import jax.numpy as jnp
from jax import lax
from jax.sharding import Mesh, PartitionSpec as P

HEAD_DIM = 64
EPSILON = 1e-06
SCORE_SCALE = 0.125
HIGHEST = lax.Precision.HIGHEST
F32 = jnp.float32
BF16 = jnp.bfloat16

WIDE = ("z", "q", "h")
CHIPS = ("h", "pipe")
PARTS = ("q", "tp")
SWAP = [(0, 1), (1, 0)]


def dot(left, right, contract, precision=None):
    return lax.dot_general(
        left, right, (contract, ((), ())), precision=precision, preferred_element_type=F32
    )


def mm(left, right):
    return dot(left, right, ((1,), (0,)))


def mm_nt(left, right):
    return dot(left, right, ((1,), (1,)))


def mm_tn(left, right):
    return dot(left, right, ((0,), (0,)))


def swapped(values, axis):
    return lax.ppermute(values, axis, SWAP)


def exchanged(values, axes):
    return lax.all_to_all(values, axes, split_axis=0, concat_axis=0, tiled=True)


def norm_rows(values, gain_vector):
    inverse = lax.rsqrt(jnp.mean(values * values, axis=-1, keepdims=True) + EPSILON)
    return (inverse, (values * inverse * gain_vector).astype(BF16))


def norm_back(values, inverse, gain_vector, grad_normed):
    scaled = grad_normed * gain_vector
    grad_values = inverse * scaled - values * (inverse * inverse * inverse) * jnp.mean(
        scaled * values, axis=-1, keepdims=True
    )
    grad_gain = jnp.sum(grad_normed * values * inverse, axis=0)
    return (grad_values, grad_gain)


def sum_parts(values):
    if lax.axis_size("q") == 1:
        mine = lax.axis_index("tp")
        kept = lax.dynamic_index_in_dim(values, mine, 0, keepdims=False)
        other = lax.dynamic_index_in_dim(values, 1 - mine, 0, keepdims=False)
        got = swapped(other.astype(BF16), "tp")
        return kept.astype(F32) + got.astype(F32)
    return jnp.sum(exchanged(values.astype(BF16), PARTS).astype(F32), axis=0)


def sum_chips(values):
    chunks = exchanged(values.astype(BF16).reshape(4, -1, values.shape[-1]), CHIPS)
    return jnp.sum(chunks.astype(F32), axis=0)


def gather_weights(query_weight, key_weight, value_weight, output_weight, extras):
    rows, cols = query_weight.shape
    half, group = (rows // 2, cols // 2)
    packed = jnp.stack([query_weight, key_weight, value_weight, output_weight.T])
    packed = packed.reshape(4, 2, half, 2, group).transpose(1, 3, 2, 0, 4)
    by_core = exchanged(packed, "tp").reshape(4, half, 4 * group)
    small = jnp.broadcast_to(extras[None], (4,) + extras.shape)
    by_chip = exchanged(jnp.concatenate([by_core, small], axis=-1), CHIPS)
    width = by_chip.shape[-1]
    by_chip = by_chip.reshape(2, 2, half, width)
    whole = []
    for section in range(2):
        own = by_chip[:, section]
        gathered = lax.all_gather(own, ("z", "q"), axis=0, tiled=False)
        gathered = lax.all_gather(gathered, "tp", axis=2, tiled=False)
        whole.append(gathered.reshape(-1, width))
    return whole


def scatter_grads(section_grads, group, extra):
    sums = []
    for grad_w_qkv, grad_w_out, grad_small in section_grads:
        grad_small = jnp.pad(grad_small, ((0, 0), (0, extra - grad_small.shape[-1])))
        grads = jnp.concatenate([grad_w_qkv, grad_w_out, grad_small], axis=-1)
        width = grads.shape[-1]
        places = lax.axis_size("z") * lax.axis_size("q")
        split = grads.astype(BF16).reshape(places * 2, 2, -1, width)
        mine = lax.axis_index("tp")
        kept = lax.dynamic_index_in_dim(split, mine, 1, keepdims=False)
        got = swapped(lax.dynamic_index_in_dim(split, 1 - mine, 1, keepdims=False), "tp")
        both = (kept.astype(F32) + got.astype(F32)).astype(BF16)
        both = both.reshape(places, 2, -1, width)
        moved = exchanged(both, ("z", "q"))
        sums.append(jnp.sum(moved.astype(F32), axis=0).astype(BF16))
    half, width = sums[0].shape[1:]
    by_chip = exchanged(jnp.stack(sums, axis=1).reshape(4, half, width), CHIPS)
    small = jnp.sum(by_chip[:, :, 4 * group :].astype(F32), axis=0)
    by_core = exchanged(by_chip[:, :, : 4 * group].reshape(2, 2, half, 4, group), "tp")
    mats = by_core.transpose(3, 0, 2, 1, 4).reshape(4, 2 * half, 2 * group).astype(F32)
    return mats, small


def dispatch_table(routes, expert_count, most_rows):
    expert_hits = (
        routes[:, :, None] == jnp.arange(expert_count, dtype=jnp.int32)[None, None, :]
    ).astype(F32)
    order = jnp.arange(routes.shape[1])
    before = (order[:, None] > order[None, :]).astype(F32)
    ranks = jnp.einsum("tu,bue->bte", before, expert_hits)
    slot_rank = jnp.sum(ranks * expert_hits, axis=2).astype(jnp.int32)
    target_column = routes * most_rows + slot_rank
    all_columns = jnp.arange(expert_count * most_rows, dtype=jnp.int32)
    return (target_column[:, :, None] == all_columns[None, None, :]).astype(BF16)


def to_experts(table, token_rows, section):
    blocks, block_rows, columns = table.shape
    feature_dim = token_rows.shape[-1]
    grouped = token_rows.reshape(blocks, block_rows, feature_dim)
    packed = jnp.einsum("btc,btd->cbd", table, grouped, preferred_element_type=F32).astype(BF16)
    wide = lax.axis_size("z") * lax.axis_size("q") * lax.axis_size("h")
    arrived = exchanged(packed.reshape(wide, -1, feature_dim), WIDE).reshape(-1, feature_dim)
    hopped = lax.ppermute(arrived, "pipe", [(1 - section, section)])
    near = lax.all_gather(arrived, "tp", axis=0, tiled=False)
    far = lax.all_gather(hopped, "tp", axis=0, tiled=False)
    return jnp.stack([near, far], axis=1).reshape(-1, feature_dim)


def from_experts(table, slot_rows, section):
    feature_dim = slot_rows.shape[-1]
    mine = lax.axis_index("tp")
    split = slot_rows.reshape(2, 2, -1, feature_dim)
    kept = lax.dynamic_index_in_dim(split, mine, 0, keepdims=False)
    got = swapped(lax.dynamic_index_in_dim(split, 1 - mine, 0, keepdims=False), "tp")
    total = (kept.astype(F32) + got.astype(F32)).astype(BF16)
    hopped = lax.ppermute(total[1], "pipe", [(section, 1 - section)])
    back = jnp.where(lax.axis_index("pipe") == section, total[0], hopped)
    wide = lax.axis_size("z") * lax.axis_size("q") * lax.axis_size("h")
    returned = exchanged(back.reshape(wide, -1, feature_dim), WIDE)
    blocks, block_rows, columns = table.shape
    slots = returned.reshape(columns, blocks, feature_dim)
    return jnp.einsum("btc,cbd->btd", table, slots, preferred_element_type=F32).reshape(
        -1, feature_dim
    )


def split_heads(values):
    return values.reshape(values.shape[0], -1, HEAD_DIM).transpose(1, 0, 2)


def join_heads(values):
    return values.transpose(1, 0, 2).reshape(values.shape[1], -1)


def bmm(left, right, contract):
    return lax.dot_general(
        left, right, (contract, ((0,), (0,))), preferred_element_type=F32
    )


def attend(queries, keys, values):
    scores = bmm(queries, keys, ((2,), (2,))) * SCORE_SCALE
    peak = jnp.max(scores, axis=-1, keepdims=True)
    weights = jnp.exp(scores - peak)
    total = jnp.sum(weights, axis=-1, keepdims=True)
    attended = bmm(weights.astype(BF16), values, ((2,), (1,))) / total
    return attended, peak + jnp.log(total)


def attend_back(queries, keys, values, grad_attended, attended, log_total):
    delta = jnp.sum(grad_attended.astype(F32) * attended, axis=-1, keepdims=True)
    scores = bmm(queries, keys, ((2,), (2,))) * SCORE_SCALE
    probs = jnp.exp(scores - log_total)
    grad_probs = bmm(grad_attended, values, ((2,), (2,)))
    grad_scores = (probs * (grad_probs - delta)).astype(BF16)
    grad_queries = bmm(grad_scores, keys, ((2,), (1,))) * SCORE_SCALE
    grad_keys = bmm(grad_scores, queries, ((1,), (1,))) * SCORE_SCALE
    grad_values = bmm(probs.astype(BF16), grad_attended, ((1,), (1,)))
    return grad_queries, grad_keys, grad_values


def section_forward(inputs, routes, weights, w_in, w_out, section, expert_count, most_rows):
    w_qkv, w_out_rows, gain_attn, gain_moe, w_router = weights
    group = w_out_rows.shape[1]
    values_in = inputs.astype(F32)
    inverse_a, normed_a = norm_rows(values_in, gain_attn)
    rows_a = lax.all_gather(normed_a, CHIPS, axis=0, tiled=True)
    qkv = mm(rows_a, w_qkv).astype(BF16)
    kv_all = lax.all_gather(qkv[:, group:], PARTS, axis=0, tiled=True)
    queries = split_heads(qkv[:, :group])
    keys = split_heads(kv_all[:, :group])
    values = split_heads(kv_all[:, group:])
    attended, log_total = attend(queries, keys, values)
    attended_low = join_heads(attended.astype(BF16))
    hidden = values_in + sum_chips(mm_nt(attended_low, w_out_rows))
    inverse_b, normed_b = norm_rows(hidden, gain_moe)
    router_probs = jax.nn.softmax(mm(normed_b, w_router), axis=-1)
    flat_routes = routes.reshape(-1, 1)
    chosen = (flat_routes == jnp.arange(expert_count, dtype=jnp.int32)[None]).astype(F32)
    gate = jnp.sum(router_probs * chosen, axis=-1, keepdims=True)
    table = dispatch_table(routes, expert_count, most_rows)
    slots = to_experts(table, normed_b, section)
    pre_act = mm(slots, w_in)
    activated = jax.nn.gelu(pre_act).astype(BF16)
    result = mm(activated, w_out).astype(BF16)
    mixed = from_experts(table, result, section)
    output = (hidden + gate * mixed).astype(BF16)
    state = (
        values_in, inverse_a, rows_a, queries, keys, values, attended, attended_low, log_total,
        hidden, inverse_b, normed_b, router_probs, chosen, gate, mixed, table, slots, pre_act,
        activated,
    )
    return output, state


def section_backward(grad_out, state, weights, w_in, w_out, section):
    w_qkv, w_out_rows, gain_attn, gain_moe, w_router = weights
    (
        values_in, inverse_a, rows_a, queries, keys, values, attended, attended_low, log_total,
        hidden, inverse_b, normed_b, router_probs, chosen, gate, mixed, table, slots, pre_act,
        activated,
    ) = state
    grad_output = grad_out.astype(F32)
    grad_slots = to_experts(table, (gate * grad_output).astype(BF16), section)
    grad_act = mm_nt(grad_slots, w_out)
    unused_value, gelu_back = jax.vjp(jax.nn.gelu, pre_act)
    grad_pre = gelu_back(grad_act)[0].astype(BF16)
    grad_rows = mm_nt(grad_pre, w_in).astype(BF16)
    grad_gate = jnp.sum(grad_output * mixed, axis=-1, keepdims=True)
    grad_logits = gate * grad_gate * (chosen - router_probs)
    grad_router = dot(normed_b.astype(F32), grad_logits, ((0,), (0,)), HIGHEST)
    grad_normed_router = dot(grad_logits, w_router.astype(F32), ((1,), (1,)), HIGHEST)
    grad_normed_b = grad_normed_router + from_experts(table, grad_rows, section)
    grad_hidden_norm, grad_gain_moe = norm_back(hidden, inverse_b, gain_moe, grad_normed_b)
    grad_hidden = grad_output + grad_hidden_norm
    grad_hidden_rows = lax.all_gather(grad_hidden.astype(BF16), CHIPS, axis=0, tiled=True)
    grad_attended = split_heads(mm(grad_hidden_rows, w_out_rows).astype(BF16))
    grad_queries, grad_keys, grad_values = attend_back(
        queries, keys, values, grad_attended, attended, log_total
    )
    grad_kv = jnp.concatenate([join_heads(grad_keys), join_heads(grad_values)], axis=-1)
    parts = lax.axis_size("q") * lax.axis_size("tp")
    grad_kv = sum_parts(grad_kv.reshape(parts, -1, grad_kv.shape[-1]))
    grad_qkv = jnp.concatenate([join_heads(grad_queries), grad_kv], axis=-1).astype(BF16)
    grad_normed_a = sum_chips(mm_nt(grad_qkv, w_qkv))
    grad_input_norm, grad_gain_attn = norm_back(values_in, inverse_a, gain_attn, grad_normed_a)
    grad_input = (grad_hidden + grad_input_norm).astype(BF16)
    grad_w_qkv = mm_tn(rows_a, grad_qkv)
    grad_w_out = mm_tn(grad_hidden_rows, attended_low)
    small = jnp.concatenate([grad_gain_attn[:, None], grad_gain_moe[:, None], grad_router], axis=-1)
    return grad_input, (grad_w_qkv, grad_w_out, small), (slots, grad_pre, activated, grad_slots)


def shards(
    block_input,
    out_cotangent,
    routes,
    attn_gain,
    query_weight,
    key_weight,
    value_weight,
    output_weight,
    moe_gain,
    router_weight,
    expert_in,
    expert_out,
):
    micro_count, seq_count, half_rows, feature_dim = block_input.shape
    sequences = micro_count * seq_count
    expert_count = router_weight.shape[-1]
    most_rows = max(2, 3 * half_rows // (2 * expert_count))
    pipe, core = (lax.axis_index("pipe"), lax.axis_index("tp"))
    extra = -(-(2 + expert_count) // 128) * 128

    small = jnp.concatenate([attn_gain[0][:, None], moe_gain[0][:, None], router_weight[0]], axis=-1)
    small = jnp.pad(small, ((0, 0), (0, extra - small.shape[-1])))
    whole = gather_weights(
        query_weight[0], key_weight[0], value_weight[0], output_weight[0], small
    )
    group = query_weight.shape[-1] // 2

    def parts_of(array):
        return (
            array[:, : 3 * group],
            array[:, 3 * group : 4 * group],
            array[:, 4 * group].astype(F32),
            array[:, 4 * group + 1].astype(F32),
            array[:, 4 * group + 2 : 4 * group + 2 + expert_count],
        )

    weights = [parts_of(array) for array in whole]

    own_routes = lax.dynamic_slice_in_dim(
        routes[0, :, :, :, 0].reshape(sequences, -1), core * half_rows, half_rows, 1
    )
    route_rows = jnp.pad(
        own_routes.astype(BF16)[:, None, :], ((0, 0), (0, 15), (0, feature_dim - half_rows))
    )
    moved = exchanged(
        jnp.concatenate(
            [
                block_input.reshape(sequences, half_rows, feature_dim),
                out_cotangent.reshape(sequences, half_rows, feature_dim),
                route_rows,
            ],
            axis=1,
        ),
        "z",
    )
    pairs = moved.reshape(sequences // 2, 2, -1, feature_dim)
    mine = lax.dynamic_index_in_dim(pairs, pipe, 1, keepdims=False)
    inputs = mine[:, :half_rows].reshape(-1, feature_dim)
    cotangent = mine[:, half_rows : 2 * half_rows].reshape(-1, feature_dim)
    routes_here = pairs[:, :, 2 * half_rows, :half_rows]
    kept = lax.dynamic_index_in_dim(routes_here, pipe, 1, keepdims=False)
    got = swapped(lax.dynamic_index_in_dim(routes_here, 1 - pipe, 1, keepdims=False), "pipe")
    kept, got = (kept.astype(jnp.int32), got.astype(jnp.int32))
    section_routes = [jnp.where(pipe == 0, kept, got), jnp.where(pipe == 0, got, kept)]

    w_in, w_out = (expert_in[0, 0], expert_out[0, 0])
    outputs, states = ([], [])
    current = inputs
    for section in range(2):
        current, state = section_forward(
            current, section_routes[section], weights[section], w_in, w_out, section,
            expert_count, most_rows,
        )
        outputs.append(current)
        states.append(state)
    grads, expert_parts, input_grads = ([None, None], [None, None], [None, None])
    current = cotangent
    for section in (1, 0):
        current, grads[section], expert_parts[section] = section_backward(
            current, states[section], weights[section], w_in, w_out, section
        )
        input_grads[section] = current

    def to_owners(first, second):
        first, second = (v.reshape(sequences // 2, 1, half_rows, feature_dim) for v in (first, second))
        kept = jnp.where(pipe == 0, first, second)
        got = swapped(jnp.where(pipe == 0, second, first), "pipe")
        both = jnp.where(
            pipe == 0, jnp.concatenate([kept, got], axis=1), jnp.concatenate([got, kept], axis=1)
        )
        home = exchanged(both.reshape(sequences, half_rows, feature_dim), "z")
        return home.reshape(1, micro_count, seq_count, half_rows, feature_dim)

    layer_outputs = to_owners(outputs[0], outputs[1])
    grads_home = to_owners(input_grads[0], input_grads[1])

    slots, grad_pre, activated, grad_slots = (
        jnp.where(pipe == 0, first, second) for first, second in zip(*expert_parts)
    )
    grad_w_in = mm_tn(slots, grad_pre)
    grad_w_out = mm_tn(activated, grad_slots)
    mats, small = scatter_grads(grads, group, extra)
    return (
        layer_outputs,
        grads_home,
        small[:, 0][None],
        mats[0][None],
        mats[1][None],
        mats[2][None],
        mats[3].T[None],
        small[:, 1][None],
        small[:, 2 : 2 + expert_count][None],
        grad_w_in[None, None],
        grad_w_out[None, None],
    )


def solution(mesh):
    pipe, wide, tp = (mesh.shape["pipe"], mesh.shape["wide"], mesh.shape["tp"])
    planes = Mesh(mesh.devices.reshape(pipe, 4, wide // 8, 2, tp), ("pipe", "z", "q", "h", "tp"))
    rows = WIDE + ("tp",)
    placed = (
        P(None, None, rows, None),
        P(None, None, rows, None),
        P("pipe", None, None, WIDE, None),
        P("pipe", rows),
        P("pipe", WIDE, "tp"),
        P("pipe", WIDE, "tp"),
        P("pipe", WIDE, "tp"),
        P("pipe", "tp", WIDE),
        P("pipe", rows),
        P("pipe", rows, None),
        P("pipe", WIDE, None, "tp"),
        P("pipe", WIDE, "tp", None),
    )
    return jax.shard_map(
        shards,
        mesh=planes,
        in_specs=placed,
        out_specs=(
            P("pipe", None, None, rows, None),
            P("pipe", None, None, rows, None),
            P("pipe", rows),
            P("pipe", WIDE, "tp"),
            P("pipe", WIDE, "tp"),
            P("pipe", WIDE, "tp"),
            P("pipe", "tp", WIDE),
            P("pipe", rows),
            P("pipe", rows, None),
            P("pipe", WIDE, None, "tp"),
            P("pipe", WIDE, "tp", None),
        ),
        check_vma=False,
    )
```

```python
import jax
import jax.numpy as jnp
from jax import lax
from jax.experimental import pallas as pl
from jax.experimental.pallas import tpu as pltpu
from jax.sharding import Mesh, PartitionSpec as P

HEAD_DIM = 64
EPSILON = 1e-06
SCORE_SCALE = 0.125
HIGHEST = lax.Precision.HIGHEST
F32 = jnp.float32
BF16 = jnp.bfloat16

WIDE = ("z", "q", "h")
CHIPS = ("h", "pipe")
PARTS = ("q", "tp")
SWAP = [(0, 1), (1, 0)]
VMEM_BYTES = 48 * 1024 * 1024


def dot(left, right, contract, precision=None):
    return lax.dot_general(
        left, right, (contract, ((), ())), precision=precision, preferred_element_type=F32
    )


def mm(left, right):
    return dot(left, right, ((1,), (0,)))


def mm_nt(left, right):
    return dot(left, right, ((1,), (1,)))


def mm_tn(left, right):
    return dot(left, right, ((0,), (0,)))


def swapped(values, axis):
    return lax.ppermute(values, axis, SWAP)


def exchanged(values, axes):
    return lax.all_to_all(values, axes, split_axis=0, concat_axis=0, tiled=True)


def norm_rows(values, gain_vector):
    inverse = lax.rsqrt(jnp.mean(values * values, axis=-1, keepdims=True) + EPSILON)
    return (inverse, (values * inverse * gain_vector).astype(BF16))


def norm_back(values, inverse, gain_vector, grad_normed):
    scaled = grad_normed * gain_vector
    grad_values = inverse * scaled - values * (inverse * inverse * inverse) * jnp.mean(
        scaled * values, axis=-1, keepdims=True
    )
    grad_gain = jnp.sum(grad_normed * values * inverse, axis=0)
    return (grad_values, grad_gain)


def sum_parts(values):
    if lax.axis_size("q") == 1:
        mine = lax.axis_index("tp")
        kept = lax.dynamic_index_in_dim(values, mine, 0, keepdims=False)
        other = lax.dynamic_index_in_dim(values, 1 - mine, 0, keepdims=False)
        got = swapped(other.astype(BF16), "tp")
        return kept.astype(F32) + got.astype(F32)
    return jnp.sum(exchanged(values.astype(BF16), PARTS).astype(F32), axis=0)


def sum_chips(values):
    chunks = exchanged(values.astype(BF16).reshape(4, -1, values.shape[-1]), CHIPS)
    return jnp.sum(chunks.astype(F32), axis=0)


def after(value, *others):
    return lax.optimization_barrier((value,) + others)[0]


def from_z(values):
    places = lax.axis_size("z") * lax.axis_size("q")
    return exchanged(jnp.broadcast_to(values[None], (places,) + values.shape), ("z", "q"))


def spread_weights(query_weight, key_weight, value_weight, output_weight, extras):
    rows, cols = query_weight.shape
    half, group = (rows // 2, cols // 2)
    packed = jnp.stack([query_weight, key_weight, value_weight, output_weight.T])
    packed = packed.reshape(4, 2, half, 2, group).transpose(1, 3, 2, 0, 4)
    by_core = exchanged(packed, "tp").reshape(4, half, 4 * group)
    small = jnp.broadcast_to(extras[None], (4,) + extras.shape)
    by_chip = exchanged(jnp.concatenate([by_core, small], axis=-1), CHIPS)
    return by_chip.reshape(2, 2, half, -1)


def gather_section(own):
    mine = from_z(own)
    other = swapped(mine, "tp")
    core = lax.axis_index("tp")
    low, high = (jnp.where(core == 0, mine, other), jnp.where(core == 0, other, mine))
    return jnp.stack([low, high], axis=2).reshape(-1, own.shape[-1])


def scatter_start(grads):
    width = grads.shape[-1]
    places = lax.axis_size("z") * lax.axis_size("q")
    split = grads.reshape(places * 2, 2, -1, width)
    mine = lax.axis_index("tp")
    kept = lax.dynamic_index_in_dim(split, mine, 1, keepdims=False)
    got = swapped(lax.dynamic_index_in_dim(split, 1 - mine, 1, keepdims=False), "tp")
    both = (kept.astype(F32) + got.astype(F32)).astype(BF16)
    moved = exchanged(both.reshape(places, 2, -1, width), ("z", "q"))
    return jnp.sum(moved.astype(F32), axis=0).astype(BF16)


def scatter_end(sums):
    half, width = sums[0].shape[1:]
    group = width // 4
    by_chip = exchanged(jnp.stack(sums, axis=1).reshape(4, half, width), CHIPS)
    by_core = exchanged(by_chip.reshape(2, 2, half, 4, group), "tp")
    return by_core.transpose(3, 0, 2, 1, 4).reshape(4, 2 * half, 2 * group).astype(F32)


def dispatch_table(routes, expert_count, most_rows):
    blocks, block_rows = routes.shape
    expert_hits = (
        routes[:, :, None] == jnp.arange(expert_count, dtype=jnp.int32)[None, None, :]
    ).astype(F32)
    order = jnp.arange(block_rows)
    before = (order[:, None] > order[None, :]).astype(F32)
    ranks = jnp.einsum("tu,bue->bte", before, expert_hits)
    slot_rank = jnp.sum(ranks * expert_hits, axis=2).astype(jnp.int32)
    place = jnp.arange(blocks, dtype=jnp.int32)[:, None] * most_rows + slot_rank
    target = (routes * (blocks * most_rows) + place).reshape(-1)
    slots = jnp.arange(expert_count * blocks * most_rows, dtype=jnp.int32)
    return (slots[:, None] == target[None, :]).astype(BF16)


def to_experts(packed, section):
    arrived = exchanged(packed, WIDE)
    hopped = lax.ppermute(arrived, "pipe", [(1 - section, section)])
    near = lax.all_gather(arrived, "tp", axis=0, tiled=False)
    far = lax.all_gather(hopped, "tp", axis=0, tiled=False)
    return jnp.stack([near, far], axis=1)


def from_experts(results, section):
    mine = lax.axis_index("tp")
    kept = lax.dynamic_index_in_dim(results, mine, 0, keepdims=False)
    got = swapped(lax.dynamic_index_in_dim(results, 1 - mine, 0, keepdims=False), "tp")
    total = (kept.astype(F32) + got.astype(F32)).astype(BF16)
    hopped = lax.ppermute(total[1], "pipe", [(section, 1 - section)])
    back = jnp.where(lax.axis_index("pipe") == section, total[0], hopped)
    return exchanged(back, WIDE)


def whole_call(kernel, out_shape, *operands, flops=0, exps=0):
    moved = sum(v.size * v.dtype.itemsize for v in operands)
    return pl.pallas_call(
        kernel,
        out_shape=out_shape,
        compiler_params=pltpu.CompilerParams(vmem_limit_bytes=VMEM_BYTES),
        cost_estimate=pl.CostEstimate(flops=flops, bytes_accessed=moved, transcendentals=exps),
    )(*operands)


def flipped(values):
    return values.astype(F32).T.astype(BF16)


def attend_kernel(queries, keys_values, w_out_rows, part, attended, attended_flat, log_total):
    group = queries.shape[1]
    queries_flat = flipped(queries[...]) * SCORE_SCALE
    values_flat = flipped(keys_values[:, group:])
    for head in range(group // HEAD_DIM):
        lanes = slice(head * HEAD_DIM, (head + 1) * HEAD_DIM)
        scores = mm(keys_values[:, lanes], queries_flat[lanes])
        peak = jnp.max(scores, axis=0, keepdims=True)
        weights = jnp.exp(scores - peak)
        total = jnp.sum(weights, axis=0, keepdims=True)
        attended_flat[lanes, :] = mm(values_flat[lanes], weights.astype(BF16)) / total
        log_total[head : head + 1, :] = peak + jnp.log(total)
    attended[...] = attended_flat[...].T.astype(BF16)
    part[...] = mm_nt(attended[...], w_out_rows[...]).astype(BF16)


def attend(queries, keys_values, w_out_rows):
    rows, group = queries.shape
    keys = keys_values.shape[0]
    return whole_call(
        attend_kernel,
        (
            jax.ShapeDtypeStruct((rows, w_out_rows.shape[0]), BF16),
            jax.ShapeDtypeStruct((rows, group), BF16),
            jax.ShapeDtypeStruct((group, rows), F32),
            jax.ShapeDtypeStruct((8, rows), F32),
        ),
        queries,
        keys_values,
        w_out_rows,
        flops=4 * rows * keys * group,
        exps=rows * keys * group // HEAD_DIM,
    )


def attend_back_kernel(
    grad_rows, w_out_rows, queries, keys_values, attended_flat, log_total, grad_queries, grad_kv
):
    group = queries.shape[1]
    keys = keys_values.shape[0]
    chunk = min(512, keys)
    queries_flat = flipped(queries[...]) * SCORE_SCALE
    keys_flat = flipped(keys_values[:, :group])
    grad_flat = dot(w_out_rows[...], grad_rows[...], ((0,), (1,))).astype(BF16)
    products = grad_flat.astype(F32) * attended_flat[...]
    grad_queries_flat = []
    for head in range(group // HEAD_DIM):
        lanes = slice(head * HEAD_DIM, (head + 1) * HEAD_DIM)
        value_lanes = slice(group + head * HEAD_DIM, group + (head + 1) * HEAD_DIM)
        delta = jnp.sum(products[lanes], axis=0, keepdims=True)
        level = log_total[head : head + 1, :]
        query, grad = (queries_flat[lanes], grad_flat[lanes])
        own = jnp.zeros((HEAD_DIM, queries.shape[0]), F32)
        for begin in range(0, keys, chunk):
            here = slice(begin, begin + chunk)
            probs = jnp.exp(mm(keys_values[here, lanes], query) - level)
            grad_probs = mm(keys_values[here, value_lanes], grad)
            grad_scores = (probs * (grad_probs - delta)).astype(BF16)
            grad_kv[here, lanes] = mm_nt(grad_scores, query).astype(BF16)
            grad_kv[here, value_lanes] = mm_nt(probs.astype(BF16), grad).astype(BF16)
            own = own + mm(keys_flat[lanes, here], grad_scores)
        grad_queries_flat.append(own * SCORE_SCALE)
    grad_queries[...] = jnp.concatenate(grad_queries_flat, axis=0).T.astype(BF16)


def attend_back(grad_rows, w_out_rows, queries, keys_values, attended_flat, log_total):
    rows, group = queries.shape
    keys = keys_values.shape[0]
    return whole_call(
        attend_back_kernel,
        (
            jax.ShapeDtypeStruct((rows, group), BF16),
            jax.ShapeDtypeStruct((keys, 2 * group), BF16),
        ),
        grad_rows,
        w_out_rows,
        queries,
        keys_values,
        attended_flat,
        log_total,
        flops=10 * rows * keys * group,
        exps=rows * keys * group // HEAD_DIM,
    )


def attention_forward(inputs, weights):
    w_qkv, w_out_rows, gain_attn = weights[:3]
    group = w_out_rows.shape[1]
    values_in = inputs.astype(F32)
    inverse_a, normed_a = norm_rows(values_in, gain_attn)
    rows_a = lax.all_gather(normed_a, CHIPS, axis=0, tiled=True)
    qkv = mm(rows_a, w_qkv).astype(BF16)
    queries = qkv[:, :group]
    keys_values = lax.all_gather(qkv[:, group:], PARTS, axis=0, tiled=True)
    part, attended, attended_flat, log_total = attend(queries, keys_values, w_out_rows)
    hidden = values_in + sum_chips(part)
    kept = (values_in, inverse_a, rows_a, queries, keys_values, attended, attended_flat, log_total)
    return hidden, kept


def attention_backward(grad_hidden, kept, weights, first):
    w_qkv, w_out_rows, gain_attn = weights[:3]
    values_in, inverse_a, rows_a, queries, keys_values, attended, attended_flat, log_total = kept
    low, first = lax.optimization_barrier((grad_hidden.astype(BF16), first))
    grad_rows = lax.all_gather(low, CHIPS, axis=0, tiled=True)
    grad_queries, grad_kv = attend_back(
        grad_rows, w_out_rows, queries, keys_values, attended_flat, log_total
    )
    parts = lax.axis_size("q") * lax.axis_size("tp")
    grad_kv = sum_parts(grad_kv.reshape(parts, -1, grad_kv.shape[-1])).astype(BF16)
    grad_qkv = jnp.concatenate([grad_queries, grad_kv], axis=-1)
    grad_normed_a = sum_chips(mm_nt(grad_qkv, w_qkv))
    grad_input_norm, grad_gain = norm_back(values_in, inverse_a, gain_attn, grad_normed_a)
    grads = jnp.concatenate(
        [mm_tn(rows_a, grad_qkv).astype(BF16), mm_tn(grad_rows, attended).astype(BF16)], axis=-1
    )
    return (grad_hidden + grad_input_norm).astype(BF16), (grad_gain, grads), first


def route_tokens(hidden, routes, weights, expert_count, most_rows):
    gain_moe, w_router = weights[3:]
    inverse_b, normed_b = norm_rows(hidden, gain_moe)
    router_probs = jax.nn.softmax(mm(normed_b, w_router), axis=-1)
    chosen = (
        routes.reshape(-1, 1) == jnp.arange(expert_count, dtype=jnp.int32)[None]
    ).astype(F32)
    gate = jnp.sum(router_probs * chosen, axis=-1, keepdims=True)
    return inverse_b, normed_b, router_probs, chosen, gate


def pack_rows(table, rows):
    wide = lax.axis_size("z") * lax.axis_size("q") * lax.axis_size("h")
    return mm(table, rows).astype(BF16).reshape(wide, -1, rows.shape[-1])


def unpack_rows(table, returned):
    return mm_tn(table, returned.reshape(table.shape[0], -1))


def experts_forward(slots, w_in, w_out):
    pre_act = mm(slots.reshape(-1, slots.shape[-1]), w_in)
    activated = jax.nn.gelu(pre_act).astype(BF16)
    return pre_act, activated, mm(activated, w_out).astype(BF16).reshape(slots.shape)


def experts_backward(grad_slots, pre_act, w_in, w_out):
    grad_act = mm_nt(grad_slots.reshape(-1, grad_slots.shape[-1]), w_out)
    unused_value, gelu_back = jax.vjp(jax.nn.gelu, pre_act)
    grad_pre = gelu_back(grad_act)[0].astype(BF16)
    return grad_pre, mm_nt(grad_pre, w_in).astype(BF16).reshape(grad_slots.shape)


def router_backward(grad_output, mixed, routed, weights, hidden, grad_rows):
    gain_moe, w_router = weights[3:]
    inverse_b, normed_b, router_probs, chosen, gate = routed
    grad_gate = jnp.sum(grad_output * mixed, axis=-1, keepdims=True)
    grad_logits = gate * grad_gate * (chosen - router_probs)
    grad_router = dot(grad_logits, normed_b.astype(F32), ((0,), (0,)), HIGHEST)
    grad_normed_router = dot(grad_logits, w_router.astype(F32), ((1,), (1,)), HIGHEST)
    grad_normed_b = grad_normed_router + grad_rows
    grad_hidden_norm, grad_gain = norm_back(hidden, inverse_b, gain_moe, grad_normed_b)
    return grad_output + grad_hidden_norm, grad_gain, grad_router


def shards(
    block_input,
    out_cotangent,
    routes,
    attn_gain,
    query_weight,
    key_weight,
    value_weight,
    output_weight,
    moe_gain,
    router_weight,
    expert_in,
    expert_out,
):
    micro_count, seq_count, half_rows, feature_dim = block_input.shape
    sequences = micro_count * seq_count
    expert_count = router_weight.shape[-1]
    most_rows = max(2, 3 * half_rows // (2 * expert_count))
    pipe, core = (lax.axis_index("pipe"), lax.axis_index("tp"))
    extra = -(-(2 + expert_count) // 128) * 128

    own_routes = lax.dynamic_slice_in_dim(
        routes[0, :, :, :, 0].reshape(sequences, -1), core * half_rows, half_rows, 1
    ).astype(BF16)
    other_routes = swapped(own_routes, "pipe")
    route_rows = jnp.stack(
        [
            jnp.where(pipe == 0, own_routes, other_routes),
            jnp.where(pipe == 0, other_routes, own_routes),
        ],
        axis=1,
    )
    route_rows = jnp.pad(route_rows, ((0, 0), (0, 14), (0, feature_dim - half_rows)))

    def to_planes(values):
        moved = exchanged(values, "z")
        pairs = moved.reshape(sequences // 2, 2, -1, feature_dim)
        return lax.dynamic_index_in_dim(pairs, pipe, 1, keepdims=False)

    here = to_planes(
        jnp.concatenate(
            [block_input.reshape(sequences, half_rows, feature_dim), route_rows], axis=1
        )
    )
    inputs = here[:, :half_rows].reshape(-1, feature_dim)
    section_routes = [
        here[:, half_rows + section, :half_rows].astype(jnp.int32) for section in range(2)
    ]

    small = jnp.concatenate([attn_gain[0][:, None], moe_gain[0][:, None], router_weight[0]], axis=-1)
    small = jnp.pad(small, ((0, 0), (0, extra - small.shape[-1])))
    spread = spread_weights(
        query_weight[0], key_weight[0], value_weight[0], output_weight[0], small
    )
    group = query_weight.shape[-1] // 2

    def parts_of(array):
        return (
            array[:, : 3 * group],
            array[:, 3 * group : 4 * group],
            array[:, 4 * group].astype(F32),
            array[:, 4 * group + 1].astype(F32),
            array[:, 4 * group + 2 : 4 * group + 2 + expert_count],
        )

    whole = gather_section(spread[:, 0])
    weights = [parts_of(whole), None]
    w_in, w_out = (expert_in[0, 0], expert_out[0, 0])

    hidden, kept_attn = attention_forward(inputs, weights[0])
    later = gather_section(after(spread[:, 1], whole))
    cotangent = to_planes(
        after(out_cotangent.reshape(sequences, half_rows, feature_dim), kept_attn[2])
    ).reshape(-1, feature_dim)
    routed = route_tokens(hidden, section_routes[0], weights[0], expert_count, most_rows)
    table = dispatch_table(section_routes[0], expert_count, most_rows)
    slots = to_experts(pack_rows(table, routed[1]), 0)
    pre_act, activated, result = experts_forward(slots, w_in, w_out)
    mixed = unpack_rows(table, from_experts(result, 0))
    first_output = (hidden + routed[4] * mixed).astype(BF16)
    first = (hidden, kept_attn, routed, table, slots, pre_act, activated, mixed)

    weights[1] = parts_of(later)
    hidden, kept_attn = attention_forward(first_output, weights[1])
    routed = route_tokens(hidden, section_routes[1], weights[1], expert_count, most_rows)
    table = dispatch_table(section_routes[1], expert_count, most_rows)
    grad_output = cotangent.astype(F32)
    both = jnp.concatenate(
        [
            pack_rows(table, routed[1]),
            pack_rows(table, (routed[4] * grad_output).astype(BF16)),
        ],
        axis=1,
    )
    arrived = to_experts(both, 1)
    count = both.shape[1] // 2
    slots, grad_slots = (arrived[..., :count, :], arrived[..., count:, :])
    pre_act, activated, result = experts_forward(slots, w_in, w_out)
    grad_pre, grad_rows = experts_backward(grad_slots, pre_act, w_in, w_out)
    returned = from_experts(jnp.concatenate([result, grad_rows], axis=-2), 1)
    mixed = unpack_rows(table, returned[:, :count])
    second_output = (hidden + routed[4] * mixed).astype(BF16)
    expert_parts = [None, (slots, grad_pre, activated, grad_slots)]

    def to_owners(first, second, small=None):
        first, second = (v.reshape(sequences // 2, 1, half_rows, feature_dim) for v in (first, second))
        kept, sent = (jnp.where(pipe == 0, first, second), jnp.where(pipe == 0, second, first))
        if small is not None:
            kept_small = jnp.where(pipe == 0, small[0], small[1])
            sent_small = jnp.where(pipe == 0, small[1], small[0]).astype(BF16)
            sent = jnp.concatenate([sent.reshape(-1, feature_dim), sent_small], axis=0)
        got = swapped(sent, "pipe")
        if small is not None:
            kept_small = kept_small + got[-kept_small.shape[0] :].astype(F32)
            got = got[: -kept_small.shape[0]].reshape(first.shape)
        both = jnp.where(
            pipe == 0, jnp.concatenate([kept, got], axis=1), jnp.concatenate([got, kept], axis=1)
        ).reshape(sequences, half_rows, feature_dim)
        if small is None:
            home = exchanged(both, "z")
        else:
            count, planes = (kept_small.shape[0], lax.axis_size("z"))
            by_plane = kept_small.astype(BF16).reshape(count, planes, -1).transpose(1, 0, 2)
            by_plane = jnp.pad(by_plane, ((0, 0), (0, 0), (0, feature_dim - by_plane.shape[-1])))
            moved = exchanged(jnp.concatenate([both, by_plane], axis=1), "z")
            home = moved[:, :half_rows]
            sums = jnp.sum(moved[:, half_rows:, : feature_dim // planes].astype(F32), axis=0)
            rest = lax.axis_size("q") * lax.axis_size("h") * lax.axis_size("tp")
            by_rest = sums.astype(BF16).reshape(count, rest, -1).transpose(1, 0, 2)
            small = jnp.sum(exchanged(by_rest, ("q", "h", "tp")).astype(F32), axis=0)
        return home.reshape(1, micro_count, seq_count, half_rows, feature_dim), small

    def small_rows(grad_gain_attn, grad_gain_moe, grad_router):
        stacked = jnp.concatenate([grad_gain_attn[None], grad_gain_moe[None], grad_router], axis=0)
        return jnp.pad(stacked, ((0, -stacked.shape[0] % 16), (0, 0)))

    grad_hidden, grad_gain_moe, grad_router = router_backward(
        grad_output, mixed, routed, weights[1], hidden, unpack_rows(table, returned[:, count:])
    )
    second_grad, (grad_gain_attn, grads), unused = attention_backward(
        grad_hidden, kept_attn, weights[1], grad_gain_moe
    )
    small_second = small_rows(grad_gain_attn, grad_gain_moe, grad_router)
    layer_outputs, unused = to_owners(first_output, second_output)
    sums_second = scatter_start(grads)

    hidden, kept_attn, routed, table, slots, pre_act, activated, mixed = first
    grad_output = second_grad.astype(F32)
    grad_slots = to_experts(pack_rows(table, (routed[4] * grad_output).astype(BF16)), 0)
    grad_pre, grad_rows = experts_backward(grad_slots, pre_act, w_in, w_out)
    expert_parts[0] = (slots, grad_pre, activated, grad_slots)
    grad_hidden, grad_gain_moe, grad_router = router_backward(
        grad_output, mixed, routed, weights[0], hidden, unpack_rows(table, from_experts(grad_rows, 0))
    )
    first_grad, (grad_gain_attn, grads), (layer_outputs, sums_second) = attention_backward(
        grad_hidden, kept_attn, weights[0], (layer_outputs, sums_second)
    )
    small_first = small_rows(grad_gain_attn, grad_gain_moe, grad_router)
    sums_first = scatter_start(grads)
    grads_home, small = to_owners(first_grad, second_grad, (small_first, small_second))

    slots, grad_pre, activated, grad_slots = (
        jnp.where(pipe == 0, first, second).reshape(-1, first.shape[-1])
        for first, second in zip(*expert_parts)
    )
    grad_w_in = mm_tn(slots, grad_pre)
    grad_w_out = mm_tn(activated, grad_slots)
    mats = scatter_end([sums_first, sums_second])
    return (
        layer_outputs,
        grads_home,
        small[0][None],
        mats[0][None],
        mats[1][None],
        mats[2][None],
        mats[3].T[None],
        small[1][None],
        small[2 : 2 + expert_count].T[None],
        grad_w_in[None, None],
        grad_w_out[None, None],
    )


def solution(mesh):
    pipe, wide, tp = (mesh.shape["pipe"], mesh.shape["wide"], mesh.shape["tp"])
    planes = Mesh(mesh.devices.reshape(pipe, 4, wide // 8, 2, tp), ("pipe", "z", "q", "h", "tp"))
    rows = WIDE + ("tp",)
    placed = (
        P(None, None, rows, None),
        P(None, None, rows, None),
        P("pipe", None, None, WIDE, None),
        P("pipe", rows),
        P("pipe", WIDE, "tp"),
        P("pipe", WIDE, "tp"),
        P("pipe", WIDE, "tp"),
        P("pipe", "tp", WIDE),
        P("pipe", rows),
        P("pipe", rows, None),
        P("pipe", WIDE, None, "tp"),
        P("pipe", WIDE, "tp", None),
    )
    return jax.shard_map(
        shards,
        mesh=planes,
        in_specs=placed,
        out_specs=(
            P("pipe", None, None, rows, None),
            P("pipe", None, None, rows, None),
            P("pipe", rows),
            P("pipe", WIDE, "tp"),
            P("pipe", WIDE, "tp"),
            P("pipe", WIDE, "tp"),
            P("pipe", "tp", WIDE),
            P("pipe", rows),
            P("pipe", rows, None),
            P("pipe", WIDE, None, "tp"),
            P("pipe", WIDE, "tp", None),
        ),
        check_vma=False,
    )
```

```python
import jax
import jax.numpy as jnp
from jax import lax
from jax.experimental import pallas as pl
from jax.experimental.pallas import tpu as pltpu
from jax.sharding import Mesh, PartitionSpec as P

HEAD_DIM = 64
EPSILON = 1e-06
SCORE_SCALE = 0.125
HIGHEST = lax.Precision.HIGHEST
F32 = jnp.float32
BF16 = jnp.bfloat16

WIDE = ("z", "q", "h")
CHIPS = ("h", "pipe")
SWAP = [(0, 1), (1, 0)]
VMEM_BYTES = 48 * 1024 * 1024


def dot(left, right, contract, precision=None):
    return lax.dot_general(
        left, right, (contract, ((), ())), precision=precision, preferred_element_type=F32
    )


def mm(left, right):
    return dot(left, right, ((1,), (0,)))


def mm_nt(left, right):
    return dot(left, right, ((1,), (1,)))


def mm_tn(left, right):
    return dot(left, right, ((0,), (0,)))


def swapped(values, axis):
    return lax.ppermute(values, axis, SWAP)


def exchanged(values, axes):
    return lax.all_to_all(values, axes, split_axis=0, concat_axis=0, tiled=True)


def norm_rows(values, gain_vector):
    inverse = lax.rsqrt(jnp.mean(values * values, axis=-1, keepdims=True) + EPSILON)
    return (inverse, (values * inverse * gain_vector).astype(BF16))


def norm_back(values, inverse, gain_vector, grad_normed):
    scaled = grad_normed * gain_vector
    grad_values = inverse * scaled - values * (inverse * inverse * inverse) * jnp.mean(
        scaled * values, axis=-1, keepdims=True
    )
    grad_gain = jnp.sum(grad_normed * values * inverse, axis=0)
    return (grad_values, grad_gain)


def gather_parts(values):
    if lax.axis_size("q") > 1:
        values = lax.all_gather(values, "q", axis=0, tiled=True)
    return values, swapped(values, "tp")


def sum_parts(own, other):
    got = swapped(other, "tp")
    places = lax.axis_size("q")
    if places == 1:
        return [own, got]
    split = (own.astype(F32) + got.astype(F32)).astype(BF16).reshape(places, -1, own.shape[-1])
    return [jnp.sum(exchanged(split, "q").astype(F32), axis=0).astype(BF16)]


def xor_z(values):
    z = lax.axis_index("z")
    values = jnp.where((z & 1) == 1, values[jnp.array([1, 0, 3, 2])], values)
    return jnp.where((z & 2) == 2, values[jnp.array([2, 3, 0, 1])], values)


def exchanged_z(values):
    mine = xor_z(values)
    parts = [mine[0]]
    for k in range(1, 4):
        parts.append(lax.ppermute(mine[k], "z", [(z, z ^ k) for z in range(4)]))
    return xor_z(jnp.stack(parts))


def to_planes(values):
    z, y = (lax.axis_index("z"), lax.axis_index("pipe"))
    mine = xor_z(values)
    got = [mine[0]]
    for k in range(1, 4):
        pairs = [(4 * p + a, 4 * p + (a ^ k)) for p in range(2) for a in range(4) if a & 1 == p]
        got.append(lax.ppermute(mine[k], ("pipe", "z"), pairs))
    own = (z & 1) == y
    near, far = (jnp.where(own, got[0], got[1]), jnp.where(own, got[2], got[3]))
    near_at = jnp.where(own, z, z ^ 1)
    return jnp.where(near_at == y, jnp.stack([near, far]), jnp.stack([far, near]))


def sum_chips(values):
    chunks = exchanged(values.astype(BF16).reshape(4, -1, values.shape[-1]), CHIPS)
    return jnp.sum(chunks.astype(F32), axis=0)


def after(value, *others):
    return lax.optimization_barrier((value,) + others)[0]


def from_z(values):
    places = lax.axis_size("z") * lax.axis_size("q")
    return exchanged(jnp.broadcast_to(values[None], (places,) + values.shape), ("z", "q"))


def spread_weights(query_weight, key_weight, value_weight, output_weight, extras, first):
    rows, cols = query_weight.shape
    half, group = (rows // 2, cols // 2)
    packed = jnp.stack([query_weight, key_weight, value_weight, output_weight.T])
    packed = packed.reshape(4, 2, half, 2, group).transpose(1, 3, 2, 0, 4)
    by_core = exchanged(packed, "tp").reshape(4, half, 4 * group)
    small = jnp.broadcast_to(extras[None], (4,) + extras.shape)
    by_chip = exchanged(after(jnp.concatenate([by_core, small], axis=-1), first), CHIPS)
    return by_chip.reshape(2, 2, half, -1)


def join_section(mine):
    other = swapped(mine, "tp")
    core = lax.axis_index("tp")
    low, high = (jnp.where(core == 0, mine, other), jnp.where(core == 0, other, mine))
    return jnp.stack([low, high], axis=2).reshape(-1, mine.shape[-1])


def gather_later(own):
    gathered = lax.all_gather(own, ("z", "q", "tp"), axis=0, tiled=False)
    places = lax.axis_size("z") * lax.axis_size("q")
    gathered = gathered.reshape((places, 2) + own.shape).transpose(0, 2, 1, 3, 4)
    return gathered.reshape(-1, own.shape[-1])


def scatter_start(grads):
    width = grads.shape[-1]
    places = lax.axis_size("z") * lax.axis_size("q")
    split = grads.reshape(places * 2, 2, -1, width)
    mine = lax.axis_index("tp")
    kept = lax.dynamic_index_in_dim(split, mine, 1, keepdims=False)
    got = swapped(lax.dynamic_index_in_dim(split, 1 - mine, 1, keepdims=False), "tp")
    both = (kept.astype(F32) + got.astype(F32)).astype(BF16)
    moved = exchanged(both.reshape(places, 2, -1, width), ("z", "q"))
    return jnp.sum(moved.astype(F32), axis=0).astype(BF16)


def scatter_later(grads):
    width = grads.shape[-1]
    places = lax.axis_size("z") * lax.axis_size("q")
    split = grads.reshape(places, 2, 2, -1, width).transpose(0, 2, 1, 3, 4)
    half = split.shape[3]
    sums = lax.psum_scatter(
        split.reshape(-1, width), ("z", "q", "tp"), scatter_dimension=0, tiled=True
    )
    return sums.reshape(2, half, width)


def scatter_chips(sums):
    half, width = sums[0].shape[1:]
    return exchanged(jnp.stack(sums, axis=1).reshape(4, half, width), CHIPS)


def scatter_end(by_chip):
    half, width = by_chip.shape[1:]
    group = width // 4
    by_core = exchanged(by_chip.reshape(2, 2, half, 4, group), "tp")
    return by_core.transpose(3, 0, 2, 1, 4).reshape(4, 2 * half, 2 * group).astype(F32)


def dispatch_table(routes, expert_count, most_rows):
    blocks, block_rows = routes.shape
    expert_hits = (
        routes[:, :, None] == jnp.arange(expert_count, dtype=jnp.int32)[None, None, :]
    ).astype(F32)
    order = jnp.arange(block_rows)
    before = (order[:, None] > order[None, :]).astype(F32)
    ranks = jnp.einsum("tu,bue->bte", before, expert_hits)
    slot_rank = jnp.sum(ranks * expert_hits, axis=2).astype(jnp.int32)
    place = jnp.arange(blocks, dtype=jnp.int32)[:, None] * most_rows + slot_rank
    target = (routes * (blocks * most_rows) + place).reshape(-1)
    slots = jnp.arange(expert_count * blocks * most_rows, dtype=jnp.int32)
    return (slots[:, None] == target[None, :]).astype(BF16)


def to_experts(packed):
    pipe = lax.axis_index("pipe")
    count = [rows for rows in packed if rows is not None][0].shape[1]
    arrived = exchanged(jnp.concatenate([r for r in packed if r is not None], axis=1), WIDE)
    if packed[1] is None:
        kept, got = (arrived, lax.ppermute(arrived, "pipe", [(1, 0)]))
    elif packed[0] is None:
        kept, got = (arrived, lax.ppermute(arrived, "pipe", [(0, 1)]))
    else:
        first, second = (arrived[:, :count], arrived[:, count:])
        kept, sent = (jnp.where(pipe == 0, first, second), jnp.where(pipe == 0, second, first))
        got = swapped(sent, "pipe")
    rows = [kept, swapped(kept, "tp"), got, swapped(got, "tp")]
    return jnp.stack(rows).reshape((2, 2) + kept.shape)


def from_experts(results, sections):
    got = swapped(results[:, 1], "tp")
    near, far = ((results[k, 0].astype(F32) + got[k].astype(F32)).astype(BF16) for k in range(2))
    pipe = lax.axis_index("pipe")
    if len(sections) == 2:
        hopped = swapped(far, "pipe")
        back = jnp.where(
            pipe == 0,
            jnp.concatenate([near, hopped], axis=1),
            jnp.concatenate([hopped, near], axis=1),
        )
    else:
        hopped = lax.ppermute(far, "pipe", [(sections[0], 1 - sections[0])])
        back = jnp.where(pipe == sections[0], near, hopped)
    return exchanged(back, WIDE)


def whole_call(kernel, out_shape, *operands, flops=0, exps=0):
    moved = sum(v.size * v.dtype.itemsize for v in operands)
    return pl.pallas_call(
        kernel,
        out_shape=out_shape,
        compiler_params=pltpu.CompilerParams(vmem_limit_bytes=VMEM_BYTES),
        cost_estimate=pl.CostEstimate(flops=flops, bytes_accessed=moved, transcendentals=exps),
    )(*operands)


def flipped(values):
    return values.astype(F32).T.astype(BF16)


def attend_kernel(own, own_parts, other_parts, whole, part, attended, attended_flat, log_total):
    group = own.shape[1] // 3
    queries_flat = flipped(own[:, :group]) * SCORE_SCALE
    sides = (own_parts, other_parts)
    values_flat = [flipped(side[:, 2 * group :]) for side in sides]
    for head in range(group // HEAD_DIM):
        lanes = slice(head * HEAD_DIM, (head + 1) * HEAD_DIM)
        key_lanes = slice(group + head * HEAD_DIM, group + (head + 1) * HEAD_DIM)
        scores = [mm(side[:, key_lanes], queries_flat[lanes]) for side in sides]
        peak = jnp.maximum(*(jnp.max(block, axis=0, keepdims=True) for block in scores))
        weights = [jnp.exp(block - peak) for block in scores]
        total = sum(jnp.sum(block, axis=0, keepdims=True) for block in weights)
        summed = sum(mm(flat[lanes], block.astype(BF16)) for flat, block in zip(values_flat, weights))
        attended_flat[lanes, :] = summed / total
        log_total[head : head + 1, :] = peak + jnp.log(total)
    attended[...] = attended_flat[...].T.astype(BF16)
    part[...] = mm_nt(attended[...], whole[:, 3 * group : 4 * group]).astype(BF16)


def attend(own, own_parts, other_parts, whole):
    rows, group = (own.shape[0], own.shape[1] // 3)
    keys = 2 * own_parts.shape[0]
    return whole_call(
        attend_kernel,
        (
            jax.ShapeDtypeStruct((rows, whole.shape[0]), BF16),
            jax.ShapeDtypeStruct((rows, group), BF16),
            jax.ShapeDtypeStruct((group, rows), F32),
            jax.ShapeDtypeStruct((8, rows), F32),
        ),
        own,
        own_parts,
        other_parts,
        whole,
        flops=4 * rows * keys * group,
        exps=rows * keys * group // HEAD_DIM,
    )


def attend_back_kernel(
    grad_rows, whole, own, own_parts, other_parts, attended_flat, log_total,
    grad_queries, grad_own, grad_other,
):
    group = own.shape[1] // 3
    keys = own_parts.shape[0]
    chunk = min(512, keys)
    queries_flat = flipped(own[:, :group]) * SCORE_SCALE
    w_out_rows = whole[:, 3 * group : 4 * group]
    grad_flat = dot(w_out_rows, grad_rows[...], ((0,), (1,))).astype(BF16)
    products = grad_flat.astype(F32) * attended_flat[...]
    sides = ((own_parts, grad_own), (other_parts, grad_other))
    keys_flat = [flipped(side[:, group : 2 * group]) for side, unused in sides]
    grad_queries_flat = []
    for head in range(group // HEAD_DIM):
        lanes = slice(head * HEAD_DIM, (head + 1) * HEAD_DIM)
        key_lanes = slice(group + head * HEAD_DIM, group + (head + 1) * HEAD_DIM)
        value_lanes = slice(2 * group + head * HEAD_DIM, 2 * group + (head + 1) * HEAD_DIM)
        delta = jnp.sum(products[lanes], axis=0, keepdims=True)
        level = log_total[head : head + 1, :]
        query, grad = (queries_flat[lanes], grad_flat[lanes])
        total = jnp.zeros((HEAD_DIM, own.shape[0]), F32)
        for (side, grad_side), flat in zip(sides, keys_flat):
            for begin in range(0, keys, chunk):
                here = slice(begin, begin + chunk)
                probs = jnp.exp(mm(side[here, key_lanes], query) - level)
                grad_probs = mm(side[here, value_lanes], grad)
                grad_scores = (probs * (grad_probs - delta)).astype(BF16)
                grad_side[here, lanes] = mm_nt(grad_scores, query).astype(BF16)
                grad_side[here, key_lanes] = mm_nt(probs.astype(BF16), grad).astype(BF16)
                total = total + mm(flat[lanes, here], grad_scores)
        grad_queries_flat.append(total * SCORE_SCALE)
    grad_queries[...] = jnp.concatenate(grad_queries_flat, axis=0).T.astype(BF16)


def attend_back(grad_rows, whole, own, own_parts, other_parts, attended_flat, log_total):
    rows, group = (own.shape[0], own.shape[1] // 3)
    keys = own_parts.shape[0]
    return whole_call(
        attend_back_kernel,
        (
            jax.ShapeDtypeStruct((rows, group), BF16),
            jax.ShapeDtypeStruct((keys, 2 * group), BF16),
            jax.ShapeDtypeStruct((keys, 2 * group), BF16),
        ),
        grad_rows,
        whole,
        own,
        own_parts,
        other_parts,
        attended_flat,
        log_total,
        flops=20 * rows * keys * group,
        exps=2 * rows * keys * group // HEAD_DIM,
    )


def project_kernel(rows, whole, qkv):
    qkv[...] = mm(rows[...], whole[:, : qkv.shape[1]]).astype(BF16)


def project(rows, whole, width):
    return whole_call(
        project_kernel,
        jax.ShapeDtypeStruct((rows.shape[0], width), BF16),
        rows,
        whole,
        flops=2 * rows.size * width,
    )


def project_back_kernel(grad_queries, *refs):
    *terms, whole, grad_qkv, part = refs
    grad_kv = sum(term[...].astype(F32) for term in terms).astype(BF16)
    grad_qkv[...] = jnp.concatenate([grad_queries[...], grad_kv], axis=1)
    part[...] = mm_nt(grad_qkv[...], whole[:, : grad_qkv.shape[1]]).astype(BF16)


def project_back(grad_queries, terms, whole):
    rows, width = (grad_queries.shape[0], 3 * grad_queries.shape[1])
    return whole_call(
        project_back_kernel,
        (
            jax.ShapeDtypeStruct((rows, width), BF16),
            jax.ShapeDtypeStruct((rows, whole.shape[0]), BF16),
        ),
        grad_queries,
        *terms,
        whole,
        flops=2 * rows * width * whole.shape[0],
    )


def weight_grads_kernel(rows, grad_rows, grad_qkv, attended, grads):
    grads[...] = jnp.concatenate(
        [mm_tn(rows[...], grad_qkv[...]), mm_tn(grad_rows[...], attended[...])], axis=1
    ).astype(BF16)


def weight_grads(rows, grad_rows, grad_qkv, attended):
    width = grad_qkv.shape[1] + attended.shape[1]
    return whole_call(
        weight_grads_kernel,
        jax.ShapeDtypeStruct((rows.shape[1], width), BF16),
        rows,
        grad_rows,
        grad_qkv,
        attended,
        flops=2 * rows.size * width,
    )


def attention_forward(inputs, weights):
    whole, gain_attn = weights[:2]
    values_in = inputs.astype(F32)
    inverse_a, normed_a = norm_rows(values_in, gain_attn)
    rows_a = lax.all_gather(normed_a, CHIPS, axis=0, tiled=True)
    qkv = project(rows_a, whole, 3 * weights[2])
    own_parts, other_parts = gather_parts(qkv)
    part, attended, attended_flat, log_total = attend(qkv, own_parts, other_parts, whole)
    hidden = values_in + sum_chips(part)
    kept = (
        values_in, inverse_a, rows_a, qkv, own_parts, other_parts, attended, attended_flat, log_total
    )
    return hidden, kept


def attention_backward(grad_hidden, kept, weights):
    whole, gain_attn = weights[:2]
    (
        values_in, inverse_a, rows_a, qkv, own_parts, other_parts, attended, attended_flat, log_total
    ) = kept
    grad_rows = lax.all_gather(grad_hidden.astype(BF16), CHIPS, axis=0, tiled=True)
    grad_queries, grad_own, grad_other = attend_back(
        grad_rows, whole, qkv, own_parts, other_parts, attended_flat, log_total
    )
    grad_qkv, part = project_back(grad_queries, sum_parts(grad_own, grad_other), whole)
    grad_normed_a = sum_chips(part)
    grad_input_norm, grad_gain = norm_back(values_in, inverse_a, gain_attn, grad_normed_a)
    grads = weight_grads(rows_a, grad_rows, grad_qkv, attended)
    return (grad_hidden + grad_input_norm).astype(BF16), (grad_gain, grads)


def route_tokens(hidden, routes, weights, expert_count, most_rows):
    gain_moe, w_router = weights[3:]
    inverse_b, normed_b = norm_rows(hidden, gain_moe)
    router_probs = jax.nn.softmax(mm(normed_b, w_router), axis=-1)
    chosen = (
        routes.reshape(-1, 1) == jnp.arange(expert_count, dtype=jnp.int32)[None]
    ).astype(F32)
    gate = jnp.sum(router_probs * chosen, axis=-1, keepdims=True)
    return inverse_b, normed_b, router_probs, chosen, gate


def pack_rows(table, rows):
    wide = lax.axis_size("z") * lax.axis_size("q") * lax.axis_size("h")
    return mm(table, rows).astype(BF16).reshape(wide, -1, rows.shape[-1])


def unpack_rows(table, returned):
    return mm_tn(table, returned.reshape(table.shape[0], -1))


def expert_trip(slots, w_in, w_out):
    rows = slots.reshape(-1, slots.shape[-1])
    pre_act = mm(rows, w_in)
    activated = jax.nn.gelu(pre_act).astype(BF16)
    result = mm(activated, w_out).astype(BF16)
    return (rows, pre_act, activated), result.reshape(slots.shape)


def expert_trip_back(grad_slots, kept, w_in, w_out, extra=None):
    rows, pre_act, activated = kept
    grad_part = grad_slots.reshape(rows.shape)
    grad_act = mm_nt(grad_part, w_out)
    unused_value, gelu_back = jax.vjp(jax.nn.gelu, pre_act)
    grad_pre = gelu_back(grad_act)[0].astype(BF16)
    grad_rows = mm_nt(grad_pre, w_in)
    if extra is not None:
        grad_rows = grad_rows + extra
    return (rows, grad_pre, activated, grad_part), grad_rows.astype(BF16).reshape(grad_slots.shape)


def expert_gate(slots, grad_slots, result, w_router):
    rows = slots.reshape(-1, slots.shape[-1])
    grad_out = grad_slots.reshape(rows.shape).astype(F32)
    expert = (lax.axis_index("z") * lax.axis_size("q") + lax.axis_index("q")) * 2 + lax.axis_index("h")
    probs = jax.nn.softmax(mm(rows, w_router), axis=-1)
    here = (jnp.arange(w_router.shape[1], dtype=jnp.int32) == expert).astype(F32)[None]
    gate = jnp.sum(probs * here, axis=-1, keepdims=True)
    grad_gate = jnp.sum(grad_out * result.reshape(rows.shape).astype(F32), axis=-1, keepdims=True)
    grad_logits = gate * grad_gate * (here - probs)
    through_router = mm_nt(grad_logits.astype(BF16), w_router)
    return (gate * grad_out).astype(BF16).reshape(slots.shape), through_router


def router_grads(grad_output, mixed, routed):
    inverse_b, normed_b, router_probs, chosen, gate = routed
    grad_gate = jnp.sum(grad_output * mixed, axis=-1, keepdims=True)
    grad_logits = gate * grad_gate * (chosen - router_probs)
    return grad_logits, dot(grad_logits, normed_b.astype(F32), ((0,), (0,)), HIGHEST)


def moe_norm_back(grad_output, grad_normed_b, hidden, routed, weights):
    grad_hidden_norm, grad_gain = norm_back(hidden, routed[0], weights[3], grad_normed_b)
    return grad_output + grad_hidden_norm, grad_gain


def shards(
    block_input,
    out_cotangent,
    routes,
    attn_gain,
    query_weight,
    key_weight,
    value_weight,
    output_weight,
    moe_gain,
    router_weight,
    expert_in,
    expert_out,
):
    micro_count, seq_count, half_rows, feature_dim = block_input.shape
    sequences = micro_count * seq_count
    expert_count = router_weight.shape[-1]
    most_rows = max(2, 3 * half_rows // (2 * expert_count))
    pipe, core = (lax.axis_index("pipe"), lax.axis_index("tp"))
    extra = -(-(2 + expert_count) // 128) * 128

    own_routes = lax.dynamic_slice_in_dim(
        routes[0, :, :, :, 0].reshape(sequences, -1), core * half_rows, half_rows, 1
    ).astype(BF16)
    other_routes = swapped(own_routes, "pipe")
    route_rows = jnp.stack(
        [
            jnp.where(pipe == 0, own_routes, other_routes),
            jnp.where(pipe == 0, other_routes, own_routes),
        ],
        axis=1,
    )
    route_rows = jnp.pad(route_rows, ((0, 0), (0, 14), (0, feature_dim - half_rows)))

    input_rows = jnp.concatenate(
        [block_input.reshape(sequences, half_rows, feature_dim), route_rows], axis=1
    )
    here = to_planes(input_rows)
    inputs = here[:, :half_rows].reshape(-1, feature_dim)
    section_routes = [
        here[:, half_rows + section, :half_rows].astype(jnp.int32) for section in range(2)
    ]

    small = jnp.concatenate([attn_gain[0][:, None], moe_gain[0][:, None], router_weight[0]], axis=-1)
    small = jnp.pad(small, ((0, 0), (0, extra - small.shape[-1])))
    spread = spread_weights(
        query_weight[0], key_weight[0], value_weight[0], output_weight[0], small, here
    )
    group = query_weight.shape[-1] // 2

    def parts_of(array):
        return (
            array,
            array[:, 4 * group].astype(F32),
            group,
            array[:, 4 * group + 1].astype(F32),
            array[:, 4 * group + 2 : 4 * group + 2 + expert_count],
        )

    whole = join_section(from_z(spread[:, 0]))
    weights = [parts_of(whole), parts_of(gather_later(spread[:, 1]))]
    w_in, w_out = (expert_in[0, 0], expert_out[0, 0])

    tables = [dispatch_table(rows, expert_count, most_rows) for rows in section_routes]
    cotangent = to_planes(out_cotangent.reshape(sequences, half_rows, feature_dim)).reshape(
        -1, feature_dim
    )
    hidden, kept_attn = attention_forward(inputs, weights[0])
    routed = route_tokens(hidden, section_routes[0], weights[0], expert_count, most_rows)
    slots = to_experts((pack_rows(tables[0], routed[1]), pack_rows(tables[1], cotangent)))
    cotangent_slots = slots
    kept_expert, result = expert_trip(slots, w_in, w_out)
    mixed = unpack_rows(tables[0], from_experts(result, (0,)))
    first_output = (hidden + routed[4] * mixed).astype(BF16)
    first = (hidden, kept_attn, routed, kept_expert, mixed)

    hidden, kept_attn = attention_forward(first_output, weights[1])
    routed = route_tokens(hidden, section_routes[1], weights[1], expert_count, most_rows)
    slots = to_experts((None, pack_rows(tables[1], routed[1])))
    kept_expert, second_result = expert_trip(slots, w_in, w_out)
    grad_slots, through_router = expert_gate(slots, cotangent_slots, second_result, weights[1][4])
    part, grad_results = expert_trip_back(grad_slots, kept_expert, w_in, w_out, through_router)
    expert_parts = [None, part]
    returned_grad = from_experts(grad_results, (1,))
    grad_output = cotangent.astype(F32)

    def to_owners(first, second, small=None, chips=None):
        first, second = (v.reshape(sequences // 2, 1, half_rows, feature_dim) for v in (first, second))
        kept, sent = (jnp.where(pipe == 0, first, second), jnp.where(pipe == 0, second, first))
        if small is not None:
            kept_small = jnp.where(pipe == 0, small[0], small[1])
            sent_small = jnp.where(pipe == 0, small[1], small[0]).astype(BF16)
            sent = jnp.concatenate([sent.reshape(-1, feature_dim), sent_small], axis=0)
        got = swapped(sent, "pipe")
        if small is not None:
            kept_small = kept_small + got[-kept_small.shape[0] :].astype(F32)
            got = got[: -kept_small.shape[0]].reshape(first.shape)
        both = jnp.where(
            pipe == 0, jnp.concatenate([kept, got], axis=1), jnp.concatenate([got, kept], axis=1)
        ).reshape(sequences, half_rows, feature_dim)
        if small is None:
            home = exchanged_z(both)
        else:
            count, planes = (kept_small.shape[0], lax.axis_size("z"))
            by_plane = kept_small.astype(BF16).reshape(count, planes, -1).transpose(1, 0, 2)
            by_plane = jnp.pad(by_plane, ((0, 0), (0, 0), (0, feature_dim - by_plane.shape[-1])))
            both = jnp.concatenate([both, by_plane], axis=1)
            chips = chips(both)
            moved = exchanged_z(both)
            home = moved[:, :half_rows]
            sums = jnp.sum(moved[:, half_rows:, : feature_dim // planes].astype(F32), axis=0)
            rest = lax.axis_size("q") * lax.axis_size("h") * lax.axis_size("tp")
            by_rest = sums.astype(BF16).reshape(count, rest, -1).transpose(1, 0, 2)
            small = jnp.sum(exchanged(after(by_rest, chips), ("q", "h", "tp")).astype(F32), axis=0)
        return home.reshape(1, micro_count, seq_count, half_rows, feature_dim), small, chips

    def small_rows(grad_gain_attn, grad_gain_moe, grad_router):
        stacked = jnp.concatenate([grad_gain_attn[None], grad_gain_moe[None], grad_router], axis=0)
        return jnp.pad(stacked, ((0, -stacked.shape[0] % 16), (0, 0)))

    grad_hidden, grad_gain_moe = moe_norm_back(
        grad_output, unpack_rows(tables[1], returned_grad), hidden, routed, weights[1]
    )
    second_grad, (grad_gain_attn, grads) = attention_backward(grad_hidden, kept_attn, weights[1])
    sums_second = scatter_later(grads)
    second = (hidden, routed, grad_output, grad_gain_attn, grad_gain_moe)

    hidden, kept_attn, routed, kept_expert, mixed = first
    grad_output = second_grad.astype(F32)
    grad_slots = to_experts((pack_rows(tables[0], (routed[4] * grad_output).astype(BF16)), None))
    expert_parts[0], grad_results = expert_trip_back(grad_slots, kept_expert, w_in, w_out)
    grad_logits, grad_router = router_grads(grad_output, mixed, routed)
    grad_normed_router = mm_nt(grad_logits.astype(BF16), weights[0][4])
    slots, grad_pre, activated, grad_part = (
        jnp.where(pipe == 0, low, high) for low, high in zip(*expert_parts)
    )
    grad_w_in = mm_tn(slots, grad_pre)
    grad_w_out = mm_tn(activated, grad_part)
    returned = from_experts(jnp.where(pipe == 0, grad_results, second_result), (0, 1))
    count = returned.shape[1] // 2
    grad_hidden, grad_gain_moe = moe_norm_back(
        grad_output,
        grad_normed_router + unpack_rows(tables[0], returned[:, :count]),
        hidden,
        routed,
        weights[0],
    )
    hidden, routed, grad_output, *gains = second
    mixed = unpack_rows(tables[1], returned[:, count:])
    second_output = (hidden + routed[4] * mixed).astype(BF16)
    small_second = small_rows(*gains, router_grads(grad_output, mixed, routed)[1])
    layer_outputs = to_owners(first_output, second_output)[0]
    grad_hidden, grad_w_in, grad_w_out = lax.optimization_barrier(
        (grad_hidden, grad_w_in, grad_w_out)
    )
    first_grad, (grad_gain_attn, grads) = attention_backward(grad_hidden, kept_attn, weights[0])
    small_first = small_rows(grad_gain_attn, grad_gain_moe, grad_router)
    sums_first = scatter_start(grads)
    grads_home, small, by_chip = to_owners(
        first_grad,
        second_grad,
        (small_first, small_second),
        lambda first: scatter_chips([after(sums_first, first), sums_second]),
    )
    mats = scatter_end(by_chip)
    return (
        layer_outputs,
        grads_home,
        small[0][None],
        mats[0][None],
        mats[1][None],
        mats[2][None],
        mats[3].T[None],
        small[1][None],
        small[2 : 2 + expert_count].T[None],
        grad_w_in[None, None],
        grad_w_out[None, None],
    )


def solution(mesh):
    pipe, wide, tp = (mesh.shape["pipe"], mesh.shape["wide"], mesh.shape["tp"])
    planes = Mesh(mesh.devices.reshape(pipe, 4, wide // 8, 2, tp), ("pipe", "z", "q", "h", "tp"))
    rows = WIDE + ("tp",)
    placed = (
        P(None, None, rows, None),
        P(None, None, rows, None),
        P("pipe", None, None, WIDE, None),
        P("pipe", rows),
        P("pipe", WIDE, "tp"),
        P("pipe", WIDE, "tp"),
        P("pipe", WIDE, "tp"),
        P("pipe", "tp", WIDE),
        P("pipe", rows),
        P("pipe", rows, None),
        P("pipe", WIDE, None, "tp"),
        P("pipe", WIDE, "tp", None),
    )
    return jax.shard_map(
        shards,
        mesh=planes,
        in_specs=placed,
        out_specs=(
            P("pipe", None, None, rows, None),
            P("pipe", None, None, rows, None),
            P("pipe", rows),
            P("pipe", WIDE, "tp"),
            P("pipe", WIDE, "tp"),
            P("pipe", WIDE, "tp"),
            P("pipe", "tp", WIDE),
            P("pipe", rows),
            P("pipe", rows, None),
            P("pipe", WIDE, None, "tp"),
            P("pipe", WIDE, "tp", None),
        ),
        check_vma=False,
    )
```

```python
import jax
import jax.numpy as jnp
from jax import lax
from jax.experimental import pallas as pl
from jax.experimental.pallas import tpu as pltpu
from jax.sharding import Mesh, PartitionSpec as P

HEAD_DIM = 64
EPSILON = 1e-06
SCORE_SCALE = 0.125
HIGHEST = lax.Precision.HIGHEST
F32 = jnp.float32
BF16 = jnp.bfloat16

WIDE = ("z", "q", "h")
CHIPS = ("h", "pipe")
SWAP = [(0, 1), (1, 0)]
VMEM_BYTES = 48 * 1024 * 1024


def dot(left, right, contract, precision=None):
    return lax.dot_general(
        left, right, (contract, ((), ())), precision=precision, preferred_element_type=F32
    )


def mm(left, right):
    return dot(left, right, ((1,), (0,)))


def mm_nt(left, right):
    return dot(left, right, ((1,), (1,)))


def mm_tn(left, right):
    return dot(left, right, ((0,), (0,)))


def swapped(values, axis):
    return lax.ppermute(values, axis, SWAP)


def exchanged(values, axes):
    return lax.all_to_all(values, axes, split_axis=0, concat_axis=0, tiled=True)


def norm_rows(values, gain_vector):
    inverse = lax.rsqrt(jnp.mean(values * values, axis=-1, keepdims=True) + EPSILON)
    return (inverse, (values * inverse * gain_vector).astype(BF16))


def norm_back(values, inverse, gain_vector, grad_normed):
    scaled = grad_normed * gain_vector
    grad_values = inverse * scaled - values * (inverse * inverse * inverse) * jnp.mean(
        scaled * values, axis=-1, keepdims=True
    )
    grad_gain = jnp.sum(grad_normed * values * inverse, axis=0)
    return (grad_values, grad_gain)


def gather_parts(values):
    if lax.axis_size("q") > 1:
        values = lax.all_gather(values, "q", axis=0, tiled=True)
    return values, swapped(values, "tp")


def sum_parts(own, other):
    got = swapped(other, "tp")
    places = lax.axis_size("q")
    if places == 1:
        return [own, got]
    split = (own.astype(F32) + got.astype(F32)).astype(BF16).reshape(places, -1, own.shape[-1])
    return [jnp.sum(exchanged(split, "q").astype(F32), axis=0).astype(BF16)]


def xor_z(values):
    z = lax.axis_index("z")
    odd, high = ((z & 1) == 1, (z & 2) == 2)
    a, b, c, d = (values[k] for k in range(4))
    a, b, c, d = (jnp.where(odd, b, a), jnp.where(odd, a, b), jnp.where(odd, d, c), jnp.where(odd, c, d))
    return [jnp.where(high, c, a), jnp.where(high, d, b), jnp.where(high, a, c), jnp.where(high, b, d)]


def exchanged_z(values):
    mine = xor_z(values)
    parts = [mine[0]]
    for k in range(1, 4):
        parts.append(lax.ppermute(mine[k], "z", [(z, z ^ k) for z in range(4)]))
    return jnp.stack(xor_z(parts))


def to_planes(values):
    z, y = (lax.axis_index("z"), lax.axis_index("pipe"))
    mine = xor_z(values)
    got = [mine[0]]
    for k in range(1, 4):
        pairs = [(4 * p + a, 4 * p + (a ^ k)) for p in range(2) for a in range(4) if a & 1 == p]
        got.append(lax.ppermute(mine[k], ("pipe", "z"), pairs))
    own = (z & 1) == y
    near, far = (jnp.where(own, got[0], got[1]), jnp.where(own, got[2], got[3]))
    near_at = jnp.where(own, z, z ^ 1)
    return jnp.where(near_at == y, jnp.stack([near, far]), jnp.stack([far, near]))


def sum_chips(values):
    chunks = exchanged(values.astype(BF16).reshape(4, -1, values.shape[-1]), CHIPS)
    return jnp.sum(chunks.astype(F32), axis=0)


def after(value, *others):
    return lax.optimization_barrier((value,) + others)[0]


def from_z(values):
    places = lax.axis_size("z") * lax.axis_size("q")
    return exchanged(jnp.broadcast_to(values[None], (places,) + values.shape), ("z", "q"))


def spread_weights(query_weight, key_weight, value_weight, output_weight, extras, inputs):
    rows, cols = query_weight.shape
    half, group = (rows // 2, cols // 2)
    packed = jnp.stack([query_weight, key_weight, value_weight, output_weight.T])
    packed = packed.reshape(4, 2, half, 2, group).transpose(1, 3, 2, 0, 4)
    by_core = exchanged(packed, "tp").reshape(4, half, 4 * group)
    small = jnp.broadcast_to(extras[None], (4,) + extras.shape)
    own = jnp.concatenate([by_core, small], axis=-1)
    count, width = inputs.shape
    copies = jnp.pad(inputs, ((0, 0), (0, own.shape[-1] - width)))
    copies = jnp.broadcast_to(copies[None], (4,) + copies.shape)
    by_chip = exchanged(jnp.concatenate([own, copies], axis=1), CHIPS)
    gathered = by_chip[:, half:, :width].reshape(4 * count, width)
    return by_chip[:, :half].reshape(2, 2, half, -1), gathered


def join_section(mine):
    other = swapped(mine, "tp")
    core = lax.axis_index("tp")
    low, high = (jnp.where(core == 0, mine, other), jnp.where(core == 0, other, mine))
    return jnp.stack([low, high], axis=2).reshape(-1, mine.shape[-1])


def gather_later(own):
    gathered = lax.all_gather(own, ("z", "q", "tp"), axis=0, tiled=False)
    places = lax.axis_size("z") * lax.axis_size("q")
    gathered = gathered.reshape((places, 2) + own.shape).transpose(0, 2, 1, 3, 4)
    return gathered.reshape(-1, own.shape[-1])


def scatter_later(grads):
    width = grads.shape[-1]
    places = lax.axis_size("z") * lax.axis_size("q")
    split = grads.reshape(places, 2, 2, -1, width).transpose(0, 2, 1, 3, 4)
    half = split.shape[3]
    sums = lax.psum_scatter(
        split.reshape(-1, width), ("z", "q", "tp"), scatter_dimension=0, tiled=True
    )
    return sums.reshape(2, half, width)


def scatter_chips(sums):
    half, width = sums[0].shape[1:]
    return exchanged(jnp.stack(sums, axis=1).reshape(4, half, width), CHIPS)


def scatter_end(by_chip):
    half, width = by_chip.shape[1:]
    group = width // 4
    by_core = exchanged(by_chip.reshape(2, 2, half, 4, group), "tp")
    return by_core.transpose(3, 0, 2, 1, 4).reshape(4, 2 * half, 2 * group).astype(F32)


def dispatch_table(routes, expert_count, most_rows):
    blocks, block_rows = routes.shape
    expert_hits = (
        routes[:, :, None] == jnp.arange(expert_count, dtype=jnp.int32)[None, None, :]
    ).astype(F32)
    order = jnp.arange(block_rows)
    before = (order[:, None] > order[None, :]).astype(F32)
    ranks = jnp.einsum("tu,bue->bte", before, expert_hits)
    slot_rank = jnp.sum(ranks * expert_hits, axis=2).astype(jnp.int32)
    place = jnp.arange(blocks, dtype=jnp.int32)[:, None] * most_rows + slot_rank
    target = (routes * (blocks * most_rows) + place).reshape(-1)
    slots = jnp.arange(expert_count * blocks * most_rows, dtype=jnp.int32)
    return (slots[:, None] == target[None, :]).astype(BF16)


def to_experts(packed):
    pipe = lax.axis_index("pipe")
    count = [rows for rows in packed if rows is not None][0].shape[1]
    arrived = exchanged(jnp.concatenate([r for r in packed if r is not None], axis=1), WIDE)
    if packed[1] is None:
        kept, got = (arrived, lax.ppermute(arrived, "pipe", [(1, 0)]))
    elif packed[0] is None:
        kept, got = (arrived, lax.ppermute(arrived, "pipe", [(0, 1)]))
    else:
        first, second = (arrived[:, :count], arrived[:, count:])
        kept, sent = (jnp.where(pipe == 0, first, second), jnp.where(pipe == 0, second, first))
        got = swapped(sent, "pipe")
    rows = [kept, swapped(kept, "tp"), got, swapped(got, "tp")]
    return jnp.stack(rows).reshape((2, 2) + kept.shape)


def from_experts(results, sections):
    got = swapped(results[:, 1], "tp")
    near, far = ((results[k, 0].astype(F32) + got[k].astype(F32)).astype(BF16) for k in range(2))
    pipe = lax.axis_index("pipe")
    if len(sections) == 2:
        hopped = swapped(far, "pipe")
        back = jnp.where(
            pipe == 0,
            jnp.concatenate([near, hopped], axis=1),
            jnp.concatenate([hopped, near], axis=1),
        )
    else:
        hopped = lax.ppermute(far, "pipe", [(sections[0], 1 - sections[0])])
        back = jnp.where(pipe == sections[0], near, hopped)
    return exchanged(back, WIDE)


def whole_call(kernel, out_shape, *operands, flops=0, exps=0):
    moved = sum(v.size * v.dtype.itemsize for v in operands)
    return pl.pallas_call(
        kernel,
        out_shape=out_shape,
        compiler_params=pltpu.CompilerParams(vmem_limit_bytes=VMEM_BYTES),
        cost_estimate=pl.CostEstimate(flops=flops, bytes_accessed=moved, transcendentals=exps),
    )(*operands)


def flipped(values):
    return values.astype(F32).T.astype(BF16)


def attend_kernel(queries, own, other, whole, part, attended, attended_flat, log_total):
    group = queries.shape[1]
    queries_flat = flipped(queries[...]) * SCORE_SCALE
    sides = (own, other)
    values_flat = [flipped(side[:, group:]) for side in sides]
    for head in range(group // HEAD_DIM):
        lanes = slice(head * HEAD_DIM, (head + 1) * HEAD_DIM)
        scores = [mm(side[:, lanes], queries_flat[lanes]) for side in sides]
        peak = jnp.maximum(*(jnp.max(block, axis=0, keepdims=True) for block in scores))
        weights = [jnp.exp(block - peak) for block in scores]
        total = sum(jnp.sum(block, axis=0, keepdims=True) for block in weights)
        summed = sum(mm(flat[lanes], block.astype(BF16)) for flat, block in zip(values_flat, weights))
        attended_flat[lanes, :] = summed / total
        log_total[head : head + 1, :] = peak + jnp.log(total)
    attended[...] = attended_flat[...].T.astype(BF16)
    part[...] = mm_nt(attended[...], whole[:, 3 * group : 4 * group]).astype(BF16)


def attend(queries, own, other, whole):
    rows, group = queries.shape
    keys = 2 * own.shape[0]
    return whole_call(
        attend_kernel,
        (
            jax.ShapeDtypeStruct((rows, whole.shape[0]), BF16),
            jax.ShapeDtypeStruct((rows, group), BF16),
            jax.ShapeDtypeStruct((group, rows), F32),
            jax.ShapeDtypeStruct((8, rows), F32),
        ),
        queries,
        own,
        other,
        whole,
        flops=4 * rows * keys * group,
        exps=rows * keys * group // HEAD_DIM,
    )


def attend_back_kernel(
    grad_rows, whole, queries, own, other, attended_flat, log_total,
    grad_queries, grad_own, grad_other,
):
    group = queries.shape[1]
    keys = own.shape[0]
    chunk = min(512, keys)
    queries_flat = flipped(queries[...]) * SCORE_SCALE
    w_out_rows = whole[:, 3 * group : 4 * group]
    grad_flat = dot(w_out_rows, grad_rows[...], ((0,), (1,))).astype(BF16)
    products = grad_flat.astype(F32) * attended_flat[...]
    sides = ((own, grad_own), (other, grad_other))
    keys_flat = [flipped(side[:, :group]) for side, unused in sides]
    grad_queries_flat = []
    for head in range(group // HEAD_DIM):
        lanes = slice(head * HEAD_DIM, (head + 1) * HEAD_DIM)
        value_lanes = slice(group + head * HEAD_DIM, group + (head + 1) * HEAD_DIM)
        delta = jnp.sum(products[lanes], axis=0, keepdims=True)
        level = log_total[head : head + 1, :]
        query, grad = (queries_flat[lanes], grad_flat[lanes])
        total = jnp.zeros((HEAD_DIM, queries.shape[0]), F32)
        for (side, grad_side), flat in zip(sides, keys_flat):
            for begin in range(0, keys, chunk):
                here = slice(begin, begin + chunk)
                probs = jnp.exp(mm(side[here, lanes], query) - level)
                grad_probs = mm(side[here, value_lanes], grad)
                grad_scores = (probs * (grad_probs - delta)).astype(BF16)
                grad_side[here, lanes] = mm_nt(grad_scores, query).astype(BF16)
                grad_side[here, value_lanes] = mm_nt(probs.astype(BF16), grad).astype(BF16)
                total = total + mm(flat[lanes, here], grad_scores)
        grad_queries_flat.append(total * SCORE_SCALE)
    grad_queries[...] = jnp.concatenate(grad_queries_flat, axis=0).T.astype(BF16)


def attend_back(grad_rows, whole, queries, own, other, attended_flat, log_total):
    rows, group = queries.shape
    keys = own.shape[0]
    return whole_call(
        attend_back_kernel,
        (
            jax.ShapeDtypeStruct((rows, group), BF16),
            jax.ShapeDtypeStruct((keys, 2 * group), BF16),
            jax.ShapeDtypeStruct((keys, 2 * group), BF16),
        ),
        grad_rows,
        whole,
        queries,
        own,
        other,
        attended_flat,
        log_total,
        flops=20 * rows * keys * group,
        exps=2 * rows * keys * group // HEAD_DIM,
    )


def project_kernel(rows, whole, normed, queries, keys_values, small):
    group = queries.shape[1]
    small[...] = whole[:, 4 * group :].astype(F32).T
    values = rows[...].astype(F32)
    normed[...] = norm_rows(values, small[0:1, :])[1]
    queries[...] = mm(normed[...], whole[:, :group]).astype(BF16)
    keys_values[...] = mm(normed[...], whole[:, group : 3 * group]).astype(BF16)


def project(rows, whole, group):
    count, width = rows.shape
    extra = whole.shape[1] - 4 * group
    return whole_call(
        project_kernel,
        (
            jax.ShapeDtypeStruct((count, width), BF16),
            jax.ShapeDtypeStruct((count, group), BF16),
            jax.ShapeDtypeStruct((count, 2 * group), BF16),
            jax.ShapeDtypeStruct((extra, width), F32),
        ),
        rows,
        whole,
        flops=6 * rows.size * group,
    )


def project_back_kernel(grad_queries, *refs):
    *terms, whole, grad_qkv, part = refs
    grad_kv = sum(term[...].astype(F32) for term in terms).astype(BF16)
    grad_qkv[...] = jnp.concatenate([grad_queries[...], grad_kv], axis=1)
    part[...] = mm_nt(grad_qkv[...], whole[:, : grad_qkv.shape[1]]).astype(BF16)


def project_back(grad_queries, terms, whole):
    rows, width = (grad_queries.shape[0], 3 * grad_queries.shape[1])
    return whole_call(
        project_back_kernel,
        (
            jax.ShapeDtypeStruct((rows, width), BF16),
            jax.ShapeDtypeStruct((rows, whole.shape[0]), BF16),
        ),
        grad_queries,
        *terms,
        whole,
        flops=2 * rows * width * whole.shape[0],
    )


def gelu_parts(values):
    scale, cubic = (0.7978845608028654, 0.044715)
    square = values * values
    bend = jnp.tanh(scale * values * (1.0 + cubic * square))
    half = 0.5 * (1.0 + bend)
    slope = half + 0.5 * values * (1.0 - bend * bend) * scale * (1.0 + 3.0 * cubic * square)
    return values * half, slope


ROW_BLOCK = 256


def expert_kernel(
    slots, grad_out, w_in, w_out, small, here, result, activated, grad_part, grad_pre, grad_rows
):
    experts = here.shape[1]
    router = small[2 : 2 + experts, :].astype(BF16)
    probs = jax.nn.softmax(mm_nt(slots[...], router), axis=-1)
    gate = jnp.sum(probs * here[...], axis=-1, keepdims=True)
    low, slope = gelu_parts(mm(slots[...], w_in[...]))
    activated[...] = low.astype(BF16)
    grad_part[...] = (gate * grad_out[...].astype(F32)).astype(BF16)
    grad_pre[...] = (mm_nt(grad_part[...], w_out[...]) * slope).astype(BF16)
    result[...] = mm(activated[...], w_out[...]).astype(BF16)
    grad_gate = jnp.sum(
        grad_out[...].astype(F32) * result[...].astype(F32), axis=-1, keepdims=True
    )
    grad_logits = gate * grad_gate * (here[...] - probs)
    through_router = mm(grad_logits.astype(BF16), router)
    grad_rows[...] = (mm_nt(grad_pre[...], w_in[...]) + through_router).astype(BF16)


def expert_both(slots, grad_out, w_in, w_out, small, expert_count):
    expert = (lax.axis_index("z") * lax.axis_size("q") + lax.axis_index("q")) * 2 + lax.axis_index("h")
    here = (jnp.arange(expert_count, dtype=jnp.int32) == expert).astype(F32)[None]
    rows = slots.reshape(-1, slots.shape[-1])
    count, width = rows.shape
    hidden = w_in.shape[1]
    block = ROW_BLOCK if count % ROW_BLOCK == 0 else count

    def rows_of(size):
        return pl.BlockSpec((block, size), lambda step: (step, 0))

    def whole_of(array):
        return pl.BlockSpec(array.shape, lambda step: (0, 0))

    sizes = (width, hidden, width, hidden, width)
    result, activated, grad_part, grad_pre, grad_rows = pl.pallas_call(
        expert_kernel,
        grid=(count // block,),
        in_specs=[rows_of(width), rows_of(width)] + [whole_of(a) for a in (w_in, w_out, small, here)],
        out_specs=tuple(rows_of(size) for size in sizes),
        out_shape=tuple(jax.ShapeDtypeStruct((count, size), BF16) for size in sizes),
        compiler_params=pltpu.CompilerParams(vmem_limit_bytes=VMEM_BYTES),
        cost_estimate=pl.CostEstimate(
            flops=8 * count * width * hidden, bytes_accessed=16 * count * width, transcendentals=count * hidden
        ),
    )(rows, grad_out.reshape(rows.shape), w_in, w_out, small, here)
    kept = (rows, grad_pre, activated, grad_part)
    return kept, result.reshape(slots.shape), grad_rows.reshape(slots.shape)


def weight_grads_kernel(rows, grad_rows, grad_qkv, attended, grads):
    grads[...] = jnp.concatenate(
        [mm_tn(rows[...], grad_qkv[...]), mm_tn(grad_rows[...], attended[...])], axis=1
    ).astype(BF16)


def weight_grads(rows, grad_rows, grad_qkv, attended):
    width = grad_qkv.shape[1] + attended.shape[1]
    return whole_call(
        weight_grads_kernel,
        jax.ShapeDtypeStruct((rows.shape[1], width), BF16),
        rows,
        grad_rows,
        grad_qkv,
        attended,
        flops=2 * rows.size * width,
    )


def attention_forward(inputs, gathered, whole, group):
    values_in = inputs.astype(F32)
    rows_a, queries, keys_values, small = project(gathered, whole, group)
    own, other = gather_parts(keys_values)
    part, attended, attended_flat, log_total = attend(queries, own, other, whole)
    hidden = values_in + sum_chips(part)
    kept = (values_in, rows_a, queries, own, other, attended, attended_flat, log_total)
    return hidden, small, kept


def attention_backward(grad_hidden, small, kept, whole, last):
    values_in, rows_a, queries, own, other, attended, attended_flat, log_total = kept
    grad_rows = lax.all_gather(grad_hidden.astype(BF16), CHIPS, axis=0, tiled=True)
    grad_queries, grad_own, grad_other = attend_back(
        grad_rows, whole, queries, own, other, attended_flat, log_total
    )
    grad_qkv, part = project_back(grad_queries, sum_parts(grad_own, grad_other), whole)
    grads = weight_grads(rows_a, grad_rows, grad_qkv, attended)
    grad_normed_a = sum_chips(after(part, grads) if last else part)
    sums = scatter_later(grads)
    inverse = lax.rsqrt(jnp.mean(values_in * values_in, axis=-1, keepdims=True) + EPSILON)
    grad_input_norm, grad_gain = norm_back(values_in, inverse, small[0:1], grad_normed_a)
    return (grad_hidden + grad_input_norm).astype(BF16), grad_gain, sums


def route_tokens(hidden, routes, small, expert_count):
    inverse_b, normed_b = norm_rows(hidden, small[1:2])
    router = small[2 : 2 + expert_count].astype(BF16)
    router_probs = jax.nn.softmax(mm_nt(normed_b, router), axis=-1)
    chosen = (
        routes.reshape(-1, 1) == jnp.arange(expert_count, dtype=jnp.int32)[None]
    ).astype(F32)
    gate = jnp.sum(router_probs * chosen, axis=-1, keepdims=True)
    return inverse_b, normed_b, router_probs, chosen, gate


def pack_rows(table, rows):
    wide = lax.axis_size("z") * lax.axis_size("q") * lax.axis_size("h")
    return mm(table, rows).astype(BF16).reshape(wide, -1, rows.shape[-1])


def unpack_rows(table, returned):
    return mm_tn(table, returned.reshape(table.shape[0], -1))


def expert_trip(slots, w_in, w_out):
    rows = slots.reshape(-1, slots.shape[-1])
    pre_act = mm(rows, w_in)
    activated = jax.nn.gelu(pre_act).astype(BF16)
    result = mm(activated, w_out).astype(BF16)
    return (rows, pre_act, activated), result.reshape(slots.shape)


def expert_trip_back(grad_slots, kept, w_in, w_out, extra=None):
    rows, pre_act, activated = kept
    grad_part = grad_slots.reshape(rows.shape)
    grad_act = mm_nt(grad_part, w_out)
    unused_value, gelu_back = jax.vjp(jax.nn.gelu, pre_act)
    grad_pre = gelu_back(grad_act)[0].astype(BF16)
    grad_rows = mm_nt(grad_pre, w_in)
    if extra is not None:
        grad_rows = grad_rows + extra
    return (rows, grad_pre, activated, grad_part), grad_rows.astype(BF16).reshape(grad_slots.shape)


def router_grads(grad_output, mixed, routed):
    inverse_b, normed_b, router_probs, chosen, gate = routed
    grad_gate = jnp.sum(grad_output * mixed, axis=-1, keepdims=True)
    grad_logits = gate * grad_gate * (chosen - router_probs)
    return grad_logits, dot(grad_logits, normed_b.astype(F32), ((0,), (0,)), HIGHEST)


def moe_norm_back(grad_output, grad_normed_b, hidden, routed, small):
    grad_hidden_norm, grad_gain = norm_back(hidden, routed[0], small[1:2], grad_normed_b)
    return grad_output + grad_hidden_norm, grad_gain


def shards(
    block_input,
    out_cotangent,
    routes,
    attn_gain,
    query_weight,
    key_weight,
    value_weight,
    output_weight,
    moe_gain,
    router_weight,
    expert_in,
    expert_out,
):
    micro_count, seq_count, half_rows, feature_dim = block_input.shape
    sequences = micro_count * seq_count
    expert_count = router_weight.shape[-1]
    most_rows = max(2, 3 * half_rows // (2 * expert_count))
    pipe, core = (lax.axis_index("pipe"), lax.axis_index("tp"))
    extra = -(-(2 + expert_count) // 128) * 128

    own_routes = lax.dynamic_slice_in_dim(
        routes[0, :, :, :, 0].reshape(sequences, -1), core * half_rows, half_rows, 1
    ).astype(BF16)
    other_routes = swapped(own_routes, "pipe")
    route_rows = jnp.stack(
        [
            jnp.where(pipe == 0, own_routes, other_routes),
            jnp.where(pipe == 0, other_routes, own_routes),
        ],
        axis=1,
    )
    route_rows = jnp.pad(route_rows, ((0, 0), (0, 14), (0, feature_dim - half_rows)))

    input_rows = jnp.concatenate(
        [
            block_input.reshape(sequences, half_rows, feature_dim),
            out_cotangent.reshape(sequences, half_rows, feature_dim),
            route_rows,
        ],
        axis=1,
    )
    here = to_planes(input_rows)
    cotangent = here[:, half_rows : 2 * half_rows].reshape(-1, feature_dim)
    inputs = here[:, :half_rows].reshape(-1, feature_dim)
    section_routes = [
        here[:, 2 * half_rows + section, :half_rows].astype(jnp.int32) for section in range(2)
    ]

    small = jnp.concatenate([attn_gain[0][:, None], moe_gain[0][:, None], router_weight[0]], axis=-1)
    small = jnp.pad(small, ((0, 0), (0, extra - small.shape[-1])))
    spread, gathered = spread_weights(
        query_weight[0], key_weight[0], value_weight[0], output_weight[0], small, inputs
    )
    group = query_weight.shape[-1] // 2

    first_whole = join_section(from_z(spread[:, 0]))
    whole = [first_whole, gather_later(after(spread[:, 1], first_whole))]
    w_in, w_out = (expert_in[0, 0], expert_out[0, 0])

    tables = [dispatch_table(rows, expert_count, most_rows) for rows in section_routes]
    hidden, first_small, kept_attn = attention_forward(inputs, gathered, whole[0], group)
    routed = route_tokens(hidden, section_routes[0], first_small, expert_count)
    packed, whole[1] = lax.optimization_barrier((pack_rows(tables[0], routed[1]), whole[1]))
    slots = to_experts((packed, pack_rows(tables[1], cotangent)))
    cotangent_slots = slots
    kept_expert, result = expert_trip(slots, w_in, w_out)
    mixed = unpack_rows(tables[0], from_experts(result, (0,)))
    first_output = (hidden + routed[4] * mixed).astype(BF16)
    first = (hidden, first_small, kept_attn, routed, kept_expert, mixed)

    gathered = lax.all_gather(first_output, CHIPS, axis=0, tiled=True)
    hidden, small, kept_attn = attention_forward(first_output, gathered, whole[1], group)
    routed = route_tokens(hidden, section_routes[1], small, expert_count)
    slots = to_experts((None, pack_rows(tables[1], routed[1])))
    part, second_result, grad_results = expert_both(
        slots, cotangent_slots, w_in, w_out, small, expert_count
    )
    expert_parts = [None, part]
    returned_grad = from_experts(grad_results, (1,))
    grad_output = cotangent.astype(F32)

    def by_pipe(first, second):
        return jnp.where(pipe == 0, first, second), jnp.where(pipe == 0, second, first)

    def paired(kept, got):
        return jnp.stack(by_pipe(kept, got), axis=1).reshape(sequences, -1, feature_dim)

    def to_owners(outputs, grads, small, sums):
        kept, sent = by_pipe(*grads)
        kept_small, sent_small = by_pipe(*small)
        count = kept_small.shape[0]
        got = swapped(jnp.concatenate([sent, sent_small.astype(BF16)], axis=0), "pipe")
        kept_small = kept_small + got[-count:].astype(F32)
        shape = (sequences // 2, half_rows, feature_dim)
        planes = lax.axis_size("z")
        by_plane = kept_small.astype(BF16).reshape(count, planes, -1).transpose(1, 0, 2)
        by_plane = jnp.pad(by_plane, ((0, 0), (0, 0), (0, feature_dim - by_plane.shape[-1])))
        both = jnp.concatenate(
            [outputs, paired(kept.reshape(shape), got[:-count].reshape(shape)), by_plane], axis=1
        )
        both, *sums = lax.optimization_barrier((both, *sums))
        chips = scatter_chips(sums)
        moved = exchanged_z(both)
        total = jnp.sum(moved[:, -count:, : feature_dim // planes].astype(F32), axis=0)
        rest = lax.axis_size("q") * lax.axis_size("h") * lax.axis_size("tp")
        by_rest = total.astype(BF16).reshape(count, rest, -1).transpose(1, 0, 2)
        small = jnp.sum(exchanged(after(by_rest, chips), ("q", "h", "tp")).astype(F32), axis=0)
        return moved, small, chips

    def small_rows(grad_gain_attn, grad_gain_moe, grad_router):
        stacked = jnp.concatenate([grad_gain_attn[None], grad_gain_moe[None], grad_router], axis=0)
        return jnp.pad(stacked, ((0, -stacked.shape[0] % 16), (0, 0)))

    grad_hidden, grad_gain_moe = moe_norm_back(
        grad_output, unpack_rows(tables[1], returned_grad), hidden, routed, small
    )
    second_grad, grad_gain_attn, sums_second = attention_backward(
        grad_hidden, small, kept_attn, whole[1], False
    )
    second = (hidden, routed, grad_output, grad_gain_attn, grad_gain_moe)

    hidden, small, kept_attn, routed, kept_expert, mixed = first
    grad_output = second_grad.astype(F32)
    grad_slots = to_experts((pack_rows(tables[0], (routed[4] * grad_output).astype(BF16)), None))
    expert_parts[0], grad_results = expert_trip_back(grad_slots, kept_expert, w_in, w_out)
    grad_logits, grad_router = router_grads(grad_output, mixed, routed)
    router = small[2 : 2 + expert_count].astype(BF16)
    grad_normed_router = mm(grad_logits.astype(BF16), router)
    slots, grad_pre, activated, grad_part = (
        jnp.where(pipe == 0, low, high) for low, high in zip(*expert_parts)
    )
    grad_w_in = mm_tn(slots, grad_pre)
    grad_w_out = mm_tn(activated, grad_part)
    returned = from_experts(jnp.where(pipe == 0, grad_results, second_result), (0, 1))
    count = returned.shape[1] // 2
    grad_hidden, grad_gain_moe = moe_norm_back(
        grad_output,
        grad_normed_router + unpack_rows(tables[0], returned[:, :count]),
        hidden,
        routed,
        small,
    )
    hidden, routed, grad_output, *gains = second
    mixed = unpack_rows(tables[1], returned[:, count:])
    second_output = (hidden + routed[4] * mixed).astype(BF16)
    small_second = small_rows(*gains, router_grads(grad_output, mixed, routed)[1])
    shape = (sequences // 2, half_rows, feature_dim)
    kept_output, sent_output = by_pipe(first_output, second_output)
    outputs = paired(kept_output.reshape(shape), swapped(sent_output, "pipe").reshape(shape))
    grad_hidden, grad_w_in, grad_w_out = lax.optimization_barrier(
        (grad_hidden, grad_w_in, grad_w_out)
    )
    first_grad, grad_gain_attn, sums_first = attention_backward(
        grad_hidden, small, kept_attn, whole[0], True
    )
    small_first = small_rows(grad_gain_attn, grad_gain_moe, grad_router)
    home, small, by_chip = to_owners(
        outputs,
        (first_grad, second_grad),
        (small_first, small_second),
        (sums_first, sums_second),
    )
    layer_outputs, grads_home = (
        home[:, begin : begin + half_rows].reshape(1, micro_count, seq_count, half_rows, feature_dim)
        for begin in (0, half_rows)
    )
    mats = scatter_end(by_chip)
    return (
        layer_outputs,
        grads_home,
        small[0][None],
        mats[0][None],
        mats[1][None],
        mats[2][None],
        mats[3].T[None],
        small[1][None],
        small[2 : 2 + expert_count].T[None],
        grad_w_in[None, None],
        grad_w_out[None, None],
    )


def solution(mesh):
    pipe, wide, tp = (mesh.shape["pipe"], mesh.shape["wide"], mesh.shape["tp"])
    planes = Mesh(mesh.devices.reshape(pipe, 4, wide // 8, 2, tp), ("pipe", "z", "q", "h", "tp"))
    rows = WIDE + ("tp",)
    placed = (
        P(None, None, rows, None),
        P(None, None, rows, None),
        P("pipe", None, None, WIDE, None),
        P("pipe", rows),
        P("pipe", WIDE, "tp"),
        P("pipe", WIDE, "tp"),
        P("pipe", WIDE, "tp"),
        P("pipe", "tp", WIDE),
        P("pipe", rows),
        P("pipe", rows, None),
        P("pipe", WIDE, None, "tp"),
        P("pipe", WIDE, "tp", None),
    )
    return jax.shard_map(
        shards,
        mesh=planes,
        in_specs=placed,
        out_specs=(
            P("pipe", None, None, rows, None),
            P("pipe", None, None, rows, None),
            P("pipe", rows),
            P("pipe", WIDE, "tp"),
            P("pipe", WIDE, "tp"),
            P("pipe", WIDE, "tp"),
            P("pipe", "tp", WIDE),
            P("pipe", rows),
            P("pipe", rows, None),
            P("pipe", WIDE, None, "tp"),
            P("pipe", WIDE, "tp", None),
        ),
        check_vma=False,
    )
```

```python
import jax
import jax.numpy as jnp
from jax import lax
from jax.experimental import pallas as pl
from jax.experimental.pallas import tpu as pltpu
from jax.sharding import Mesh, PartitionSpec as P

HEAD_DIM = 64
EPSILON = 1e-06
SCORE_SCALE = 0.125
HIGHEST = lax.Precision.HIGHEST
F32 = jnp.float32
BF16 = jnp.bfloat16

WIDE = ("z", "q", "h")
CHIPS = ("h", "pipe")
SWAP = [(0, 1), (1, 0)]
VMEM_BYTES = 48 * 1024 * 1024


def dot(left, right, contract, precision=None):
    return lax.dot_general(
        left, right, (contract, ((), ())), precision=precision, preferred_element_type=F32
    )


def mm(left, right):
    return dot(left, right, ((1,), (0,)))


def mm_nt(left, right):
    return dot(left, right, ((1,), (1,)))


def mm_tn(left, right):
    return dot(left, right, ((0,), (0,)))


def swapped(values, axis):
    return lax.ppermute(values, axis, SWAP)


def exchanged(values, axes):
    return lax.all_to_all(values, axes, split_axis=0, concat_axis=0, tiled=True)


def norm_rows(values, gain_vector):
    inverse = lax.rsqrt(jnp.mean(values * values, axis=-1, keepdims=True) + EPSILON)
    return (inverse, (values * inverse * gain_vector).astype(BF16))


def norm_back(values, inverse, gain_vector, grad_normed):
    scaled = grad_normed * gain_vector
    grad_values = inverse * scaled - values * (inverse * inverse * inverse) * jnp.mean(
        scaled * values, axis=-1, keepdims=True
    )
    grad_gain = jnp.sum(grad_normed * values * inverse, axis=0)
    return (grad_values, grad_gain)


def gather_parts(values):
    if lax.axis_size("q") > 1:
        values = lax.all_gather(values, "q", axis=0, tiled=True)
    return values, swapped(values, "tp")


def sum_parts(own, other):
    got = swapped(other, "tp")
    places = lax.axis_size("q")
    if places == 1:
        return [own, got]
    split = (own.astype(F32) + got.astype(F32)).astype(BF16).reshape(places, -1, own.shape[-1])
    return [jnp.sum(exchanged(split, "q").astype(F32), axis=0).astype(BF16)]


def xor_z(values):
    z = lax.axis_index("z")
    odd, high = ((z & 1) == 1, (z & 2) == 2)
    a, b, c, d = (values[k] for k in range(4))
    a, b, c, d = (jnp.where(odd, b, a), jnp.where(odd, a, b), jnp.where(odd, d, c), jnp.where(odd, c, d))
    return [jnp.where(high, c, a), jnp.where(high, d, b), jnp.where(high, a, c), jnp.where(high, b, d)]


def exchanged_z(values):
    mine = xor_z(values)
    parts = [mine[0]]
    for k in range(1, 4):
        parts.append(lax.ppermute(mine[k], "z", [(z, z ^ k) for z in range(4)]))
    return jnp.stack(xor_z(parts))


def to_planes(values):
    z, y = (lax.axis_index("z"), lax.axis_index("pipe"))
    mine = xor_z(values)
    got = [mine[0]]
    for k in range(1, 4):
        pairs = [(4 * p + a, 4 * p + (a ^ k)) for p in range(2) for a in range(4) if a & 1 == p]
        got.append(lax.ppermute(mine[k], ("pipe", "z"), pairs))
    own = (z & 1) == y
    near, far = (jnp.where(own, got[0], got[1]), jnp.where(own, got[2], got[3]))
    near_at = jnp.where(own, z, z ^ 1)
    return jnp.where(near_at == y, jnp.stack([near, far]), jnp.stack([far, near]))


def sum_chips(values):
    chunks = exchanged(values.astype(BF16).reshape(4, -1, values.shape[-1]), CHIPS)
    return jnp.sum(chunks.astype(F32), axis=0)


def after(value, *others):
    return lax.optimization_barrier((value,) + others)[0]


def from_z(values):
    places = lax.axis_size("z") * lax.axis_size("q")
    return exchanged(jnp.broadcast_to(values[None], (places,) + values.shape), ("z", "q"))


def spread_weights(query_weight, key_weight, value_weight, output_weight, extras, inputs):
    rows, cols = query_weight.shape
    half, group = (rows // 2, cols // 2)
    packed = jnp.stack([query_weight, key_weight, value_weight, output_weight.T])
    packed = packed.reshape(4, 2, half, 2, group).transpose(1, 3, 2, 0, 4)
    by_core = exchanged(packed, "tp").reshape(4, half, 4 * group)
    small = jnp.broadcast_to(extras[None], (4,) + extras.shape)
    own = jnp.concatenate([by_core, small], axis=-1)
    count, width = inputs.shape
    copies = jnp.pad(inputs, ((0, 0), (0, own.shape[-1] - width)))
    copies = jnp.broadcast_to(copies[None], (4,) + copies.shape)
    by_chip = exchanged(jnp.concatenate([own, copies], axis=1), CHIPS)
    gathered = by_chip[:, half:, :width].reshape(4 * count, width)
    return by_chip[:, :half].reshape(2, 2, half, -1), gathered


def join_section(mine):
    other = swapped(mine, "tp")
    core = lax.axis_index("tp")
    low, high = (jnp.where(core == 0, mine, other), jnp.where(core == 0, other, mine))
    return jnp.stack([low, high], axis=2).reshape(-1, mine.shape[-1])


def gather_later(own):
    gathered = lax.all_gather(own, ("z", "q", "tp"), axis=0, tiled=False)
    places = lax.axis_size("z") * lax.axis_size("q")
    gathered = gathered.reshape((places, 2) + own.shape).transpose(0, 2, 1, 3, 4)
    return gathered.reshape(-1, own.shape[-1])


def scatter_now(grads):
    width = grads.shape[-1]
    planes = lax.axis_size("z")
    split = grads.reshape(planes * 2, 2, -1, width)
    core = lax.axis_index("tp")
    kept = lax.dynamic_index_in_dim(split, core, 1, keepdims=False)
    got = swapped(lax.dynamic_index_in_dim(split, 1 - core, 1, keepdims=False), "tp")
    both = (kept.astype(F32) + got.astype(F32)).astype(BF16)
    mine = xor_z(both.reshape(planes, 2, -1, width))
    total = mine[0].astype(F32)
    for k in range(1, planes):
        pairs = [(z, z ^ k) for z in range(planes)]
        total = total + lax.ppermute(mine[k], "z", pairs).astype(F32)
    return total.astype(BF16)


def scatter_later(grads):
    width = grads.shape[-1]
    places = lax.axis_size("z") * lax.axis_size("q")
    split = grads.reshape(places, 2, 2, -1, width).transpose(0, 2, 1, 3, 4)
    half = split.shape[3]
    sums = lax.psum_scatter(
        split.reshape(-1, width), ("z", "q", "tp"), scatter_dimension=0, tiled=True
    )
    return sums.reshape(2, half, width)


def scatter_chips(sums):
    half, width = sums[0].shape[1:]
    return exchanged(jnp.stack(sums, axis=1).reshape(4, half, width), CHIPS)


def scatter_end(by_chip):
    half, width = by_chip.shape[1:]
    group = width // 4
    by_core = exchanged(by_chip.reshape(2, 2, half, 4, group), "tp")
    return by_core.transpose(3, 0, 2, 1, 4).reshape(4, 2 * half, 2 * group).astype(F32)


def dispatch_table(routes, expert_count, most_rows):
    blocks, block_rows = routes.shape
    expert_hits = (
        routes[:, :, None] == jnp.arange(expert_count, dtype=jnp.int32)[None, None, :]
    ).astype(F32)
    order = jnp.arange(block_rows)
    before = (order[:, None] > order[None, :]).astype(F32)
    ranks = jnp.einsum("tu,bue->bte", before, expert_hits)
    slot_rank = jnp.sum(ranks * expert_hits, axis=2).astype(jnp.int32)
    place = jnp.arange(blocks, dtype=jnp.int32)[:, None] * most_rows + slot_rank
    target = (routes * (blocks * most_rows) + place).reshape(-1)
    slots = jnp.arange(expert_count * blocks * most_rows, dtype=jnp.int32)
    return (slots[:, None] == target[None, :]).astype(BF16)


def to_experts(packed):
    pipe = lax.axis_index("pipe")
    count = [rows for rows in packed if rows is not None][0].shape[1]
    arrived = exchanged(jnp.concatenate([r for r in packed if r is not None], axis=1), WIDE)
    if packed[1] is None:
        kept, got = (arrived, lax.ppermute(arrived, "pipe", [(1, 0)]))
    elif packed[0] is None:
        kept, got = (arrived, lax.ppermute(arrived, "pipe", [(0, 1)]))
    else:
        first, second = (arrived[:, :count], arrived[:, count:])
        kept, sent = (jnp.where(pipe == 0, first, second), jnp.where(pipe == 0, second, first))
        got = swapped(sent, "pipe")
    rows = [kept, swapped(kept, "tp"), got, swapped(got, "tp")]
    return jnp.stack(rows).reshape((2, 2) + kept.shape)


def from_experts(results, sections):
    got = swapped(results[:, 1], "tp")
    near, far = ((results[k, 0].astype(F32) + got[k].astype(F32)).astype(BF16) for k in range(2))
    pipe = lax.axis_index("pipe")
    if len(sections) == 2:
        hopped = swapped(far, "pipe")
        back = jnp.where(
            pipe == 0,
            jnp.concatenate([near, hopped], axis=1),
            jnp.concatenate([hopped, near], axis=1),
        )
    else:
        hopped = lax.ppermute(far, "pipe", [(sections[0], 1 - sections[0])])
        back = jnp.where(pipe == sections[0], near, hopped)
    return exchanged(back, WIDE)


def whole_call(kernel, out_shape, *operands, flops=0, exps=0):
    moved = sum(v.size * v.dtype.itemsize for v in operands)
    return pl.pallas_call(
        kernel,
        out_shape=out_shape,
        compiler_params=pltpu.CompilerParams(vmem_limit_bytes=VMEM_BYTES),
        cost_estimate=pl.CostEstimate(flops=flops, bytes_accessed=moved, transcendentals=exps),
    )(*operands)


def flipped(values):
    return values.astype(F32).T.astype(BF16)


def attend_kernel(queries, own, other, whole, part, attended, attended_flat, log_total):
    group = queries.shape[1]
    queries_flat = flipped(queries[...]) * SCORE_SCALE
    sides = (own, other)
    values_flat = [flipped(side[:, group:]) for side in sides]
    for head in range(group // HEAD_DIM):
        lanes = slice(head * HEAD_DIM, (head + 1) * HEAD_DIM)
        scores = [mm(side[:, lanes], queries_flat[lanes]) for side in sides]
        peak = jnp.maximum(*(jnp.max(block, axis=0, keepdims=True) for block in scores))
        weights = [jnp.exp(block - peak) for block in scores]
        total = sum(jnp.sum(block, axis=0, keepdims=True) for block in weights)
        summed = sum(mm(flat[lanes], block.astype(BF16)) for flat, block in zip(values_flat, weights))
        attended_flat[lanes, :] = summed / total
        log_total[head : head + 1, :] = peak + jnp.log(total)
    attended[...] = attended_flat[...].T.astype(BF16)
    part[...] = mm_nt(attended[...], whole[:, 3 * group : 4 * group]).astype(BF16)


def attend(queries, own, other, whole):
    rows, group = queries.shape
    keys = 2 * own.shape[0]
    return whole_call(
        attend_kernel,
        (
            jax.ShapeDtypeStruct((rows, whole.shape[0]), BF16),
            jax.ShapeDtypeStruct((rows, group), BF16),
            jax.ShapeDtypeStruct((group, rows), F32),
            jax.ShapeDtypeStruct((8, rows), F32),
        ),
        queries,
        own,
        other,
        whole,
        flops=4 * rows * keys * group,
        exps=rows * keys * group // HEAD_DIM,
    )


def attend_back_kernel(
    grad_rows, whole, queries, own, other, attended_flat, log_total,
    grad_queries, grad_own, grad_other,
):
    group = queries.shape[1]
    keys = own.shape[0]
    chunk = min(512, keys)
    queries_flat = flipped(queries[...]) * SCORE_SCALE
    w_out_rows = whole[:, 3 * group : 4 * group]
    grad_flat = dot(w_out_rows, grad_rows[...], ((0,), (1,))).astype(BF16)
    products = grad_flat.astype(F32) * attended_flat[...]
    sides = ((own, grad_own), (other, grad_other))
    keys_flat = [flipped(side[:, :group]) for side, unused in sides]
    grad_queries_flat = []
    for head in range(group // HEAD_DIM):
        lanes = slice(head * HEAD_DIM, (head + 1) * HEAD_DIM)
        value_lanes = slice(group + head * HEAD_DIM, group + (head + 1) * HEAD_DIM)
        delta = jnp.sum(products[lanes], axis=0, keepdims=True)
        level = log_total[head : head + 1, :]
        query, grad = (queries_flat[lanes], grad_flat[lanes])
        total = jnp.zeros((HEAD_DIM, queries.shape[0]), F32)
        for (side, grad_side), flat in zip(sides, keys_flat):
            for begin in range(0, keys, chunk):
                here = slice(begin, begin + chunk)
                probs = jnp.exp(mm(side[here, lanes], query) - level)
                grad_probs = mm(side[here, value_lanes], grad)
                grad_scores = (probs * (grad_probs - delta)).astype(BF16)
                grad_side[here, lanes] = mm_nt(grad_scores, query).astype(BF16)
                grad_side[here, value_lanes] = mm_nt(probs.astype(BF16), grad).astype(BF16)
                total = total + mm(flat[lanes, here], grad_scores)
        grad_queries_flat.append(total * SCORE_SCALE)
    grad_queries[...] = jnp.concatenate(grad_queries_flat, axis=0).T.astype(BF16)


def attend_back(grad_rows, whole, queries, own, other, attended_flat, log_total):
    rows, group = queries.shape
    keys = own.shape[0]
    return whole_call(
        attend_back_kernel,
        (
            jax.ShapeDtypeStruct((rows, group), BF16),
            jax.ShapeDtypeStruct((keys, 2 * group), BF16),
            jax.ShapeDtypeStruct((keys, 2 * group), BF16),
        ),
        grad_rows,
        whole,
        queries,
        own,
        other,
        attended_flat,
        log_total,
        flops=20 * rows * keys * group,
        exps=2 * rows * keys * group // HEAD_DIM,
    )


def project_kernel(rows, whole, normed, queries, keys_values, small):
    group = queries.shape[1]
    small[...] = whole[:, 4 * group :].astype(F32).T
    values = rows[...].astype(F32)
    normed[...] = norm_rows(values, small[0:1, :])[1]
    queries[...] = mm(normed[...], whole[:, :group]).astype(BF16)
    keys_values[...] = mm(normed[...], whole[:, group : 3 * group]).astype(BF16)


def project(rows, whole, group):
    count, width = rows.shape
    extra = whole.shape[1] - 4 * group
    return whole_call(
        project_kernel,
        (
            jax.ShapeDtypeStruct((count, width), BF16),
            jax.ShapeDtypeStruct((count, group), BF16),
            jax.ShapeDtypeStruct((count, 2 * group), BF16),
            jax.ShapeDtypeStruct((extra, width), F32),
        ),
        rows,
        whole,
        flops=6 * rows.size * group,
    )


def project_back_kernel(grad_queries, *refs):
    *terms, whole, grad_qkv, part = refs
    grad_kv = sum(term[...].astype(F32) for term in terms).astype(BF16)
    grad_qkv[...] = jnp.concatenate([grad_queries[...], grad_kv], axis=1)
    part[...] = mm_nt(grad_qkv[...], whole[:, : grad_qkv.shape[1]]).astype(BF16)


def project_back(grad_queries, terms, whole):
    rows, width = (grad_queries.shape[0], 3 * grad_queries.shape[1])
    return whole_call(
        project_back_kernel,
        (
            jax.ShapeDtypeStruct((rows, width), BF16),
            jax.ShapeDtypeStruct((rows, whole.shape[0]), BF16),
        ),
        grad_queries,
        *terms,
        whole,
        flops=2 * rows * width * whole.shape[0],
    )


def gelu_parts(values):
    scale, cubic = (0.7978845608028654, 0.044715)
    square = values * values
    bend = jnp.tanh(scale * values * (1.0 + cubic * square))
    half = 0.5 * (1.0 + bend)
    slope = half + 0.5 * values * (1.0 - bend * bend) * scale * (1.0 + 3.0 * cubic * square)
    return values * half, slope


ROW_BLOCK = 256


def expert_kernel(
    slots, grad_out, w_in, w_out, small, here, result, activated, grad_part, grad_pre, grad_rows
):
    experts = here.shape[1]
    router = small[2 : 2 + experts, :].astype(BF16)
    probs = jax.nn.softmax(mm_nt(slots[...], router), axis=-1)
    gate = jnp.sum(probs * here[...], axis=-1, keepdims=True)
    low, slope = gelu_parts(mm(slots[...], w_in[...]))
    activated[...] = low.astype(BF16)
    grad_part[...] = (gate * grad_out[...].astype(F32)).astype(BF16)
    grad_pre[...] = (mm_nt(grad_part[...], w_out[...]) * slope).astype(BF16)
    result[...] = mm(activated[...], w_out[...]).astype(BF16)
    grad_gate = jnp.sum(
        grad_out[...].astype(F32) * result[...].astype(F32), axis=-1, keepdims=True
    )
    grad_logits = gate * grad_gate * (here[...] - probs)
    through_router = mm(grad_logits.astype(BF16), router)
    grad_rows[...] = (mm_nt(grad_pre[...], w_in[...]) + through_router).astype(BF16)


def expert_both(slots, grad_out, w_in, w_out, small, expert_count):
    expert = (lax.axis_index("z") * lax.axis_size("q") + lax.axis_index("q")) * 2 + lax.axis_index("h")
    here = (jnp.arange(expert_count, dtype=jnp.int32) == expert).astype(F32)[None]
    rows = slots.reshape(-1, slots.shape[-1])
    count, width = rows.shape
    hidden = w_in.shape[1]
    block = ROW_BLOCK if count % ROW_BLOCK == 0 else count

    def rows_of(size):
        return pl.BlockSpec((block, size), lambda step: (step, 0))

    def whole_of(array):
        return pl.BlockSpec(array.shape, lambda step: (0, 0))

    sizes = (width, hidden, width, hidden, width)
    result, activated, grad_part, grad_pre, grad_rows = pl.pallas_call(
        expert_kernel,
        grid=(count // block,),
        in_specs=[rows_of(width), rows_of(width)] + [whole_of(a) for a in (w_in, w_out, small, here)],
        out_specs=tuple(rows_of(size) for size in sizes),
        out_shape=tuple(jax.ShapeDtypeStruct((count, size), BF16) for size in sizes),
        compiler_params=pltpu.CompilerParams(vmem_limit_bytes=VMEM_BYTES),
        cost_estimate=pl.CostEstimate(
            flops=8 * count * width * hidden, bytes_accessed=16 * count * width, transcendentals=count * hidden
        ),
    )(rows, grad_out.reshape(rows.shape), w_in, w_out, small, here)
    kept = (rows, grad_pre, activated, grad_part)
    return kept, result.reshape(slots.shape), grad_rows.reshape(slots.shape)


def weight_grads_kernel(rows, grad_rows, grad_qkv, attended, grads):
    grads[...] = jnp.concatenate(
        [mm_tn(rows[...], grad_qkv[...]), mm_tn(grad_rows[...], attended[...])], axis=1
    ).astype(BF16)


def weight_grads(rows, grad_rows, grad_qkv, attended):
    width = grad_qkv.shape[1] + attended.shape[1]
    return whole_call(
        weight_grads_kernel,
        jax.ShapeDtypeStruct((rows.shape[1], width), BF16),
        rows,
        grad_rows,
        grad_qkv,
        attended,
        flops=2 * rows.size * width,
    )


def attention_forward(inputs, gathered, whole, group):
    values_in = inputs.astype(F32)
    rows_a, queries, keys_values, small = project(gathered, whole, group)
    own, other = gather_parts(keys_values)
    part, attended, attended_flat, log_total = attend(queries, own, other, whole)
    hidden = values_in + sum_chips(part)
    kept = (values_in, rows_a, queries, own, other, attended, attended_flat, log_total)
    return hidden, small, kept


def attention_backward(grad_hidden, small, kept, whole, last):
    values_in, rows_a, queries, own, other, attended, attended_flat, log_total = kept
    grad_rows = lax.all_gather(grad_hidden.astype(BF16), CHIPS, axis=0, tiled=True)
    grad_queries, grad_own, grad_other = attend_back(
        grad_rows, whole, queries, own, other, attended_flat, log_total
    )
    grad_qkv, part = project_back(grad_queries, sum_parts(grad_own, grad_other), whole)
    grads = weight_grads(rows_a, grad_rows, grad_qkv, attended)
    grad_normed_a = sum_chips(after(part, grads) if last else part)
    sums = scatter_now(grads) if last and lax.axis_size("q") == 1 else scatter_later(grads)
    inverse = lax.rsqrt(jnp.mean(values_in * values_in, axis=-1, keepdims=True) + EPSILON)
    grad_input_norm, grad_gain = norm_back(values_in, inverse, small[0:1], grad_normed_a)
    return (grad_hidden + grad_input_norm).astype(BF16), grad_gain, sums


def route_tokens(hidden, routes, small, expert_count):
    inverse_b, normed_b = norm_rows(hidden, small[1:2])
    router = small[2 : 2 + expert_count].astype(BF16)
    router_probs = jax.nn.softmax(mm_nt(normed_b, router), axis=-1)
    chosen = (
        routes.reshape(-1, 1) == jnp.arange(expert_count, dtype=jnp.int32)[None]
    ).astype(F32)
    gate = jnp.sum(router_probs * chosen, axis=-1, keepdims=True)
    return inverse_b, normed_b, router_probs, chosen, gate


def pack_rows(table, rows):
    wide = lax.axis_size("z") * lax.axis_size("q") * lax.axis_size("h")
    return mm(table, rows).astype(BF16).reshape(wide, -1, rows.shape[-1])


def unpack_rows(table, returned):
    return mm_tn(table, returned.reshape(table.shape[0], -1))


def expert_trip(slots, w_in, w_out):
    rows = slots.reshape(-1, slots.shape[-1])
    pre_act = mm(rows, w_in)
    activated = jax.nn.gelu(pre_act).astype(BF16)
    result = mm(activated, w_out).astype(BF16)
    return (rows, pre_act, activated), result.reshape(slots.shape)


def expert_trip_back(grad_slots, kept, w_in, w_out, extra=None):
    rows, pre_act, activated = kept
    grad_part = grad_slots.reshape(rows.shape)
    grad_act = mm_nt(grad_part, w_out)
    unused_value, gelu_back = jax.vjp(jax.nn.gelu, pre_act)
    grad_pre = gelu_back(grad_act)[0].astype(BF16)
    grad_rows = mm_nt(grad_pre, w_in)
    if extra is not None:
        grad_rows = grad_rows + extra
    return (rows, grad_pre, activated, grad_part), grad_rows.astype(BF16).reshape(grad_slots.shape)


def router_grads(grad_output, mixed, routed):
    inverse_b, normed_b, router_probs, chosen, gate = routed
    grad_gate = jnp.sum(grad_output * mixed, axis=-1, keepdims=True)
    grad_logits = gate * grad_gate * (chosen - router_probs)
    return grad_logits, dot(grad_logits, normed_b.astype(F32), ((0,), (0,)), HIGHEST)


def moe_norm_back(grad_output, grad_normed_b, hidden, routed, small):
    grad_hidden_norm, grad_gain = norm_back(hidden, routed[0], small[1:2], grad_normed_b)
    return grad_output + grad_hidden_norm, grad_gain


def shards(
    block_input,
    out_cotangent,
    routes,
    attn_gain,
    query_weight,
    key_weight,
    value_weight,
    output_weight,
    moe_gain,
    router_weight,
    expert_in,
    expert_out,
):
    micro_count, seq_count, half_rows, feature_dim = block_input.shape
    sequences = micro_count * seq_count
    expert_count = router_weight.shape[-1]
    most_rows = max(2, 3 * half_rows // (2 * expert_count))
    pipe, core = (lax.axis_index("pipe"), lax.axis_index("tp"))
    extra = -(-(2 + expert_count) // 128) * 128

    own_routes = lax.dynamic_slice_in_dim(
        routes[0, :, :, :, 0].reshape(sequences, -1), core * half_rows, half_rows, 1
    ).astype(BF16)
    other_routes = swapped(own_routes, "pipe")
    route_rows = jnp.stack(
        [
            jnp.where(pipe == 0, own_routes, other_routes),
            jnp.where(pipe == 0, other_routes, own_routes),
        ],
        axis=1,
    )
    route_rows = jnp.pad(route_rows, ((0, 0), (0, 14), (0, feature_dim - half_rows)))

    input_rows = jnp.concatenate(
        [
            block_input.reshape(sequences, half_rows, feature_dim),
            out_cotangent.reshape(sequences, half_rows, feature_dim),
            route_rows,
        ],
        axis=1,
    )
    here = to_planes(input_rows)
    cotangent = here[:, half_rows : 2 * half_rows].reshape(-1, feature_dim)
    inputs = here[:, :half_rows].reshape(-1, feature_dim)
    section_routes = [
        here[:, 2 * half_rows + section, :half_rows].astype(jnp.int32) for section in range(2)
    ]

    small = jnp.concatenate([attn_gain[0][:, None], moe_gain[0][:, None], router_weight[0]], axis=-1)
    small = jnp.pad(small, ((0, 0), (0, extra - small.shape[-1])))
    spread, gathered = spread_weights(
        query_weight[0], key_weight[0], value_weight[0], output_weight[0], small, inputs
    )
    group = query_weight.shape[-1] // 2

    first_whole = join_section(from_z(spread[:, 0]))
    whole = [first_whole, gather_later(after(spread[:, 1], first_whole))]
    w_in, w_out = (expert_in[0, 0], expert_out[0, 0])

    tables = [dispatch_table(rows, expert_count, most_rows) for rows in section_routes]
    hidden, first_small, kept_attn = attention_forward(inputs, gathered, whole[0], group)
    routed = route_tokens(hidden, section_routes[0], first_small, expert_count)
    packed, whole[1] = lax.optimization_barrier((pack_rows(tables[0], routed[1]), whole[1]))
    slots = to_experts((packed, pack_rows(tables[1], cotangent)))
    cotangent_slots = slots
    kept_expert, result = expert_trip(slots, w_in, w_out)
    mixed = unpack_rows(tables[0], from_experts(result, (0,)))
    first_output = (hidden + routed[4] * mixed).astype(BF16)
    first = (hidden, first_small, kept_attn, routed, kept_expert, mixed)

    gathered = lax.all_gather(first_output, CHIPS, axis=0, tiled=True)
    hidden, small, kept_attn = attention_forward(first_output, gathered, whole[1], group)
    routed = route_tokens(hidden, section_routes[1], small, expert_count)
    slots = to_experts((None, pack_rows(tables[1], routed[1])))
    part, second_result, grad_results = expert_both(
        slots, cotangent_slots, w_in, w_out, small, expert_count
    )
    expert_parts = [None, part]
    returned_grad = from_experts(grad_results, (1,))
    grad_output = cotangent.astype(F32)

    def by_pipe(first, second):
        return jnp.where(pipe == 0, first, second), jnp.where(pipe == 0, second, first)

    def paired(kept, got):
        return jnp.stack(by_pipe(kept, got), axis=1).reshape(sequences, -1, feature_dim)

    def to_owners(outputs, grads, small, sums):
        kept, sent = by_pipe(*grads)
        kept_small, sent_small = by_pipe(*small)
        count = kept_small.shape[0]
        got = swapped(jnp.concatenate([sent, sent_small.astype(BF16)], axis=0), "pipe")
        kept_small = kept_small + got[-count:].astype(F32)
        shape = (sequences // 2, half_rows, feature_dim)
        planes = lax.axis_size("z")
        by_plane = kept_small.astype(BF16).reshape(count, planes, -1).transpose(1, 0, 2)
        by_plane = jnp.pad(by_plane, ((0, 0), (0, 0), (0, feature_dim - by_plane.shape[-1])))
        both = jnp.concatenate(
            [outputs, paired(kept.reshape(shape), got[:-count].reshape(shape)), by_plane], axis=1
        )
        both, *sums = lax.optimization_barrier((both, *sums))
        chips = scatter_chips(sums)
        moved = exchanged_z(both)
        total = jnp.sum(moved[:, -count:, : feature_dim // planes].astype(F32), axis=0)
        rest = lax.axis_size("q") * lax.axis_size("h") * lax.axis_size("tp")
        by_rest = total.astype(BF16).reshape(count, rest, -1).transpose(1, 0, 2)
        small = jnp.sum(exchanged(after(by_rest, chips), ("q", "h", "tp")).astype(F32), axis=0)
        return moved, small, chips

    def small_rows(grad_gain_attn, grad_gain_moe, grad_router):
        stacked = jnp.concatenate([grad_gain_attn[None], grad_gain_moe[None], grad_router], axis=0)
        return jnp.pad(stacked, ((0, -stacked.shape[0] % 16), (0, 0)))

    grad_hidden, grad_gain_moe = moe_norm_back(
        grad_output, unpack_rows(tables[1], returned_grad), hidden, routed, small
    )
    second_grad, grad_gain_attn, sums_second = attention_backward(
        grad_hidden, small, kept_attn, whole[1], False
    )
    second = (hidden, routed, grad_output, grad_gain_attn, grad_gain_moe)

    hidden, small, kept_attn, routed, kept_expert, mixed = first
    grad_output = second_grad.astype(F32)
    grad_slots = to_experts((pack_rows(tables[0], (routed[4] * grad_output).astype(BF16)), None))
    expert_parts[0], grad_results = expert_trip_back(grad_slots, kept_expert, w_in, w_out)
    grad_logits, grad_router = router_grads(grad_output, mixed, routed)
    router = small[2 : 2 + expert_count].astype(BF16)
    grad_normed_router = mm(grad_logits.astype(BF16), router)
    slots, grad_pre, activated, grad_part = (
        jnp.where(pipe == 0, low, high) for low, high in zip(*expert_parts)
    )
    grad_w_in = mm_tn(slots, grad_pre)
    grad_w_out = mm_tn(activated, grad_part)
    returned = from_experts(jnp.where(pipe == 0, grad_results, second_result), (0, 1))
    count = returned.shape[1] // 2
    grad_hidden, grad_gain_moe = moe_norm_back(
        grad_output,
        grad_normed_router + unpack_rows(tables[0], returned[:, :count]),
        hidden,
        routed,
        small,
    )
    hidden, routed, grad_output, *gains = second
    mixed = unpack_rows(tables[1], returned[:, count:])
    second_output = (hidden + routed[4] * mixed).astype(BF16)
    small_second = small_rows(*gains, router_grads(grad_output, mixed, routed)[1])
    shape = (sequences // 2, half_rows, feature_dim)
    kept_output, sent_output = by_pipe(first_output, second_output)
    outputs = paired(kept_output.reshape(shape), swapped(sent_output, "pipe").reshape(shape))
    grad_hidden, grad_w_in, grad_w_out = lax.optimization_barrier(
        (grad_hidden, grad_w_in, grad_w_out)
    )
    first_grad, grad_gain_attn, sums_first = attention_backward(
        grad_hidden, small, kept_attn, whole[0], True
    )
    small_first = small_rows(grad_gain_attn, grad_gain_moe, grad_router)
    home, small, by_chip = to_owners(
        outputs,
        (first_grad, second_grad),
        (small_first, small_second),
        (sums_first, sums_second),
    )
    layer_outputs, grads_home = (
        home[:, begin : begin + half_rows].reshape(1, micro_count, seq_count, half_rows, feature_dim)
        for begin in (0, half_rows)
    )
    mats = scatter_end(by_chip)
    return (
        layer_outputs,
        grads_home,
        small[0][None],
        mats[0][None],
        mats[1][None],
        mats[2][None],
        mats[3].T[None],
        small[1][None],
        small[2 : 2 + expert_count].T[None],
        grad_w_in[None, None],
        grad_w_out[None, None],
    )


def solution(mesh):
    pipe, wide, tp = (mesh.shape["pipe"], mesh.shape["wide"], mesh.shape["tp"])
    planes = Mesh(mesh.devices.reshape(pipe, 4, wide // 8, 2, tp), ("pipe", "z", "q", "h", "tp"))
    rows = WIDE + ("tp",)
    placed = (
        P(None, None, rows, None),
        P(None, None, rows, None),
        P("pipe", None, None, WIDE, None),
        P("pipe", rows),
        P("pipe", WIDE, "tp"),
        P("pipe", WIDE, "tp"),
        P("pipe", WIDE, "tp"),
        P("pipe", "tp", WIDE),
        P("pipe", rows),
        P("pipe", rows, None),
        P("pipe", WIDE, None, "tp"),
        P("pipe", WIDE, "tp", None),
    )
    return jax.shard_map(
        shards,
        mesh=planes,
        in_specs=placed,
        out_specs=(
            P("pipe", None, None, rows, None),
            P("pipe", None, None, rows, None),
            P("pipe", rows),
            P("pipe", WIDE, "tp"),
            P("pipe", WIDE, "tp"),
            P("pipe", WIDE, "tp"),
            P("pipe", "tp", WIDE),
            P("pipe", rows),
            P("pipe", rows, None),
            P("pipe", WIDE, None, "tp"),
            P("pipe", WIDE, "tp", None),
        ),
        check_vma=False,
    )
```

```python
import jax
import jax.numpy as jnp
from jax import lax
from jax.experimental import pallas as pl
from jax.experimental.pallas import tpu as pltpu
from jax.sharding import Mesh, PartitionSpec as P

HEAD_DIM = 64
EPSILON = 1e-06
SCORE_SCALE = 0.125
HIGHEST = lax.Precision.HIGHEST
F32 = jnp.float32
BF16 = jnp.bfloat16

WIDE = ("z", "q", "h")
CHIPS = ("h", "pipe")
SWAP = [(0, 1), (1, 0)]
VMEM_BYTES = 48 * 1024 * 1024


def dot(left, right, contract, precision=None):
    return lax.dot_general(
        left, right, (contract, ((), ())), precision=precision, preferred_element_type=F32
    )


def mm(left, right):
    return dot(left, right, ((1,), (0,)))


def mm_nt(left, right):
    return dot(left, right, ((1,), (1,)))


def mm_tn(left, right):
    return dot(left, right, ((0,), (0,)))


def swapped(values, axis):
    return lax.ppermute(values, axis, SWAP)


def exchanged_cores(values):
    core = lax.axis_index("tp")
    kept = lax.dynamic_index_in_dim(values, core, 0, keepdims=False)
    got = swapped(lax.dynamic_index_in_dim(values, 1 - core, 0, keepdims=False), "tp")
    return jnp.stack([jnp.where(core == 0, kept, got), jnp.where(core == 0, got, kept)])


def exchanged(values, axes):
    return lax.all_to_all(values, axes, split_axis=0, concat_axis=0, tiled=True)


def norm_rows(values, gain_vector):
    inverse = lax.rsqrt(jnp.mean(values * values, axis=-1, keepdims=True) + EPSILON)
    return (inverse, (values * inverse * gain_vector).astype(BF16))


def norm_back(values, inverse, gain_vector, grad_normed):
    scaled = grad_normed * gain_vector
    grad_values = inverse * scaled - values * (inverse * inverse * inverse) * jnp.mean(
        scaled * values, axis=-1, keepdims=True
    )
    grad_gain = jnp.sum(grad_normed * values * inverse, axis=0)
    return (grad_values, grad_gain)


def gather_parts(values):
    if lax.axis_size("q") > 1:
        values = lax.all_gather(values, "q", axis=0, tiled=True)
    return values, swapped(values, "tp")


def sum_parts(own, other):
    got = swapped(other, "tp")
    places = lax.axis_size("q")
    if places == 1:
        return [own, got]
    split = (own.astype(F32) + got.astype(F32)).astype(BF16).reshape(places, -1, own.shape[-1])
    return [jnp.sum(exchanged(split, "q").astype(F32), axis=0).astype(BF16)]


def xor_z(values):
    z = lax.axis_index("z")
    odd, high = ((z & 1) == 1, (z & 2) == 2)
    a, b, c, d = (values[k] for k in range(4))
    a, b, c, d = (jnp.where(odd, b, a), jnp.where(odd, a, b), jnp.where(odd, d, c), jnp.where(odd, c, d))
    return [jnp.where(high, c, a), jnp.where(high, d, b), jnp.where(high, a, c), jnp.where(high, b, d)]


def exchanged_z(values):
    mine = xor_z(values)
    parts = [mine[0]]
    for k in range(1, 4):
        parts.append(lax.ppermute(mine[k], "z", [(z, z ^ k) for z in range(4)]))
    return jnp.stack(xor_z(parts))


def to_planes(values):
    z, y = (lax.axis_index("z"), lax.axis_index("pipe"))
    mine = xor_z(values)
    got = [mine[0]]
    for k in range(1, 4):
        pairs = [(4 * p + a, 4 * p + (a ^ k)) for p in range(2) for a in range(4) if a & 1 == p]
        got.append(lax.ppermute(mine[k], ("pipe", "z"), pairs))
    own = (z & 1) == y
    near, far = (jnp.where(own, got[0], got[1]), jnp.where(own, got[2], got[3]))
    near_at = jnp.where(own, z, z ^ 1)
    return jnp.where(near_at == y, jnp.stack([near, far]), jnp.stack([far, near]))


def sum_chips(values):
    chunks = exchanged(values.astype(BF16).reshape(4, -1, values.shape[-1]), CHIPS)
    return jnp.sum(chunks.astype(F32), axis=0)


def after(value, *others):
    return lax.optimization_barrier((value,) + others)[0]


def from_z(values):
    places = lax.axis_size("z") * lax.axis_size("q")
    return exchanged(jnp.broadcast_to(values[None], (places,) + values.shape), ("z", "q"))


def spread_weights(query_weight, key_weight, value_weight, output_weight, extras, inputs):
    rows, cols = query_weight.shape
    half, group = (rows // 2, cols // 2)
    packed = jnp.stack([query_weight, key_weight, value_weight, output_weight.T])
    packed = packed.reshape(4, 2, half, 2, group).transpose(1, 3, 2, 0, 4)
    by_core = exchanged_cores(packed).reshape(4, half, 4 * group)
    small = jnp.broadcast_to(extras[None], (4,) + extras.shape)
    own = jnp.concatenate([by_core, small], axis=-1)
    count, width = inputs.shape
    copies = jnp.pad(inputs, ((0, 0), (0, own.shape[-1] - width)))
    copies = jnp.broadcast_to(copies[None], (4,) + copies.shape)
    by_chip = exchanged(jnp.concatenate([own, copies], axis=1), CHIPS)
    gathered = by_chip[:, half:, :width].reshape(4 * count, width)
    return by_chip[:, :half].reshape(2, 2, half, -1), gathered


def join_section(mine):
    other = swapped(mine, "tp")
    core = lax.axis_index("tp")
    low, high = (jnp.where(core == 0, mine, other), jnp.where(core == 0, other, mine))
    return jnp.stack([low, high], axis=2).reshape(-1, mine.shape[-1])


def gather_later(own):
    gathered = lax.all_gather(own, ("z", "q", "tp"), axis=0, tiled=False)
    places = lax.axis_size("z") * lax.axis_size("q")
    gathered = gathered.reshape((places, 2) + own.shape).transpose(0, 2, 1, 3, 4)
    return gathered.reshape(-1, own.shape[-1])


def scatter_now(grads):
    width = grads.shape[-1]
    planes = lax.axis_size("z")
    split = grads.reshape(planes * 2, 2, -1, width)
    core = lax.axis_index("tp")
    kept = lax.dynamic_index_in_dim(split, core, 1, keepdims=False)
    got = swapped(lax.dynamic_index_in_dim(split, 1 - core, 1, keepdims=False), "tp")
    both = (kept.astype(F32) + got.astype(F32)).astype(BF16)
    mine = xor_z(both.reshape(planes, 2, -1, width))
    total = mine[0].astype(F32)
    for k in range(1, planes):
        pairs = [(z, z ^ k) for z in range(planes)]
        total = total + lax.ppermute(mine[k], "z", pairs).astype(F32)
    return total.astype(BF16)


def scatter_later(grads):
    width = grads.shape[-1]
    places = lax.axis_size("z") * lax.axis_size("q")
    split = grads.reshape(places, 2, 2, -1, width).transpose(0, 2, 1, 3, 4)
    half = split.shape[3]
    sums = lax.psum_scatter(
        split.reshape(-1, width), ("z", "q", "tp"), scatter_dimension=0, tiled=True
    )
    return sums.reshape(2, half, width)


def scatter_chips(sums):
    half, width = sums[0].shape[1:]
    return exchanged(jnp.stack(sums, axis=1).reshape(4, half, width), CHIPS)


def scatter_end(by_chip):
    half, width = by_chip.shape[1:]
    group = width // 4
    by_core = exchanged_cores(by_chip.reshape(2, 2, half, 4 * group))
    by_core = by_core.reshape(2, 2, half, 4, group)
    return by_core.transpose(3, 0, 2, 1, 4).reshape(4, 2 * half, 2 * group).astype(F32)


def dispatch_table(routes, expert_count, most_rows):
    blocks, block_rows = routes.shape
    expert_hits = (
        routes[:, :, None] == jnp.arange(expert_count, dtype=jnp.int32)[None, None, :]
    ).astype(F32)
    order = jnp.arange(block_rows)
    before = (order[:, None] > order[None, :]).astype(F32)
    ranks = jnp.einsum("tu,bue->bte", before, expert_hits)
    slot_rank = jnp.sum(ranks * expert_hits, axis=2).astype(jnp.int32)
    place = jnp.arange(blocks, dtype=jnp.int32)[:, None] * most_rows + slot_rank
    target = (routes * (blocks * most_rows) + place).reshape(-1)
    slots = jnp.arange(expert_count * blocks * most_rows, dtype=jnp.int32)
    return (slots[:, None] == target[None, :]).astype(BF16)


def to_experts(packed):
    pipe = lax.axis_index("pipe")
    count = [rows for rows in packed if rows is not None][0].shape[1]
    arrived = exchanged(jnp.concatenate([r for r in packed if r is not None], axis=1), WIDE)
    if packed[1] is None:
        kept, got = (arrived, lax.ppermute(arrived, "pipe", [(1, 0)]))
    elif packed[0] is None:
        kept, got = (arrived, lax.ppermute(arrived, "pipe", [(0, 1)]))
    else:
        first, second = (arrived[:, :count], arrived[:, count:])
        kept, sent = (jnp.where(pipe == 0, first, second), jnp.where(pipe == 0, second, first))
        got = swapped(sent, "pipe")
    rows = [kept, swapped(kept, "tp"), got, swapped(got, "tp")]
    return jnp.stack(rows).reshape((2, 2) + kept.shape)


def from_experts(results, sections):
    got = swapped(results[:, 1], "tp")
    near, far = ((results[k, 0].astype(F32) + got[k].astype(F32)).astype(BF16) for k in range(2))
    pipe = lax.axis_index("pipe")
    if len(sections) == 2:
        hopped = swapped(far, "pipe")
        back = jnp.where(
            pipe == 0,
            jnp.concatenate([near, hopped], axis=1),
            jnp.concatenate([hopped, near], axis=1),
        )
    else:
        hopped = lax.ppermute(far, "pipe", [(sections[0], 1 - sections[0])])
        back = jnp.where(pipe == sections[0], near, hopped)
    return exchanged(back, WIDE)


def whole_call(kernel, out_shape, *operands, flops=0, exps=0):
    moved = sum(v.size * v.dtype.itemsize for v in operands)
    return pl.pallas_call(
        kernel,
        out_shape=out_shape,
        compiler_params=pltpu.CompilerParams(vmem_limit_bytes=VMEM_BYTES),
        cost_estimate=pl.CostEstimate(flops=flops, bytes_accessed=moved, transcendentals=exps),
    )(*operands)


def flipped(values):
    return values.astype(F32).T.astype(BF16)


def attend_kernel(queries, own, other, whole, part, attended, attended_flat, log_total):
    group = queries.shape[1]
    queries_flat = flipped(queries[...]) * SCORE_SCALE
    sides = (own, other)
    values_flat = [flipped(side[:, group:]) for side in sides]
    for head in range(group // HEAD_DIM):
        lanes = slice(head * HEAD_DIM, (head + 1) * HEAD_DIM)
        scores = [mm(side[:, lanes], queries_flat[lanes]) for side in sides]
        peak = jnp.maximum(*(jnp.max(block, axis=0, keepdims=True) for block in scores))
        weights = [jnp.exp(block - peak) for block in scores]
        total = sum(jnp.sum(block, axis=0, keepdims=True) for block in weights)
        summed = sum(mm(flat[lanes], block.astype(BF16)) for flat, block in zip(values_flat, weights))
        attended_flat[lanes, :] = summed / total
        log_total[head : head + 1, :] = peak + jnp.log(total)
    attended[...] = attended_flat[...].T.astype(BF16)
    part[...] = mm_nt(attended[...], whole[:, 3 * group : 4 * group]).astype(BF16)


def attend(queries, own, other, whole):
    rows, group = queries.shape
    keys = 2 * own.shape[0]
    return whole_call(
        attend_kernel,
        (
            jax.ShapeDtypeStruct((rows, whole.shape[0]), BF16),
            jax.ShapeDtypeStruct((rows, group), BF16),
            jax.ShapeDtypeStruct((group, rows), F32),
            jax.ShapeDtypeStruct((8, rows), F32),
        ),
        queries,
        own,
        other,
        whole,
        flops=4 * rows * keys * group,
        exps=rows * keys * group // HEAD_DIM,
    )


def attend_back_kernel(
    grad_rows, whole, queries, own, other, attended_flat, log_total,
    grad_queries, grad_own, grad_other,
):
    group = queries.shape[1]
    keys = own.shape[0]
    chunk = min(512, keys)
    queries_flat = flipped(queries[...]) * SCORE_SCALE
    w_out_rows = whole[:, 3 * group : 4 * group]
    grad_flat = dot(w_out_rows, grad_rows[...], ((0,), (1,))).astype(BF16)
    products = grad_flat.astype(F32) * attended_flat[...]
    sides = ((own, grad_own), (other, grad_other))
    keys_flat = [flipped(side[:, :group]) for side, unused in sides]
    grad_queries_flat = []
    for head in range(group // HEAD_DIM):
        lanes = slice(head * HEAD_DIM, (head + 1) * HEAD_DIM)
        value_lanes = slice(group + head * HEAD_DIM, group + (head + 1) * HEAD_DIM)
        delta = jnp.sum(products[lanes], axis=0, keepdims=True)
        level = log_total[head : head + 1, :]
        query, grad = (queries_flat[lanes], grad_flat[lanes])
        total = jnp.zeros((HEAD_DIM, queries.shape[0]), F32)
        for (side, grad_side), flat in zip(sides, keys_flat):
            for begin in range(0, keys, chunk):
                here = slice(begin, begin + chunk)
                probs = jnp.exp(mm(side[here, lanes], query) - level)
                grad_probs = mm(side[here, value_lanes], grad)
                grad_scores = (probs * (grad_probs - delta)).astype(BF16)
                grad_side[here, lanes] = mm_nt(grad_scores, query).astype(BF16)
                grad_side[here, value_lanes] = mm_nt(probs.astype(BF16), grad).astype(BF16)
                total = total + mm(flat[lanes, here], grad_scores)
        grad_queries_flat.append(total * SCORE_SCALE)
    grad_queries[...] = jnp.concatenate(grad_queries_flat, axis=0).T.astype(BF16)


def attend_back(grad_rows, whole, queries, own, other, attended_flat, log_total):
    rows, group = queries.shape
    keys = own.shape[0]
    return whole_call(
        attend_back_kernel,
        (
            jax.ShapeDtypeStruct((rows, group), BF16),
            jax.ShapeDtypeStruct((keys, 2 * group), BF16),
            jax.ShapeDtypeStruct((keys, 2 * group), BF16),
        ),
        grad_rows,
        whole,
        queries,
        own,
        other,
        attended_flat,
        log_total,
        flops=20 * rows * keys * group,
        exps=2 * rows * keys * group // HEAD_DIM,
    )


def project_kernel(rows, whole, normed, queries, keys_values, small):
    group = queries.shape[1]
    small[...] = whole[:, 4 * group :].astype(F32).T
    values = rows[...].astype(F32)
    normed[...] = norm_rows(values, small[0:1, :])[1]
    queries[...] = mm(normed[...], whole[:, :group]).astype(BF16)
    keys_values[...] = mm(normed[...], whole[:, group : 3 * group]).astype(BF16)


def project(rows, whole, group):
    count, width = rows.shape
    extra = whole.shape[1] - 4 * group
    return whole_call(
        project_kernel,
        (
            jax.ShapeDtypeStruct((count, width), BF16),
            jax.ShapeDtypeStruct((count, group), BF16),
            jax.ShapeDtypeStruct((count, 2 * group), BF16),
            jax.ShapeDtypeStruct((extra, width), F32),
        ),
        rows,
        whole,
        flops=6 * rows.size * group,
    )


def project_back_kernel(grad_queries, *refs):
    *terms, whole, grad_qkv, part = refs
    grad_kv = sum(term[...].astype(F32) for term in terms).astype(BF16)
    grad_qkv[...] = jnp.concatenate([grad_queries[...], grad_kv], axis=1)
    part[...] = mm_nt(grad_qkv[...], whole[:, : grad_qkv.shape[1]]).astype(BF16)


def project_back(grad_queries, terms, whole):
    rows, width = (grad_queries.shape[0], 3 * grad_queries.shape[1])
    return whole_call(
        project_back_kernel,
        (
            jax.ShapeDtypeStruct((rows, width), BF16),
            jax.ShapeDtypeStruct((rows, whole.shape[0]), BF16),
        ),
        grad_queries,
        *terms,
        whole,
        flops=2 * rows * width * whole.shape[0],
    )


def gelu_parts(values):
    scale, cubic = (0.7978845608028654, 0.044715)
    square = values * values
    bend = jnp.tanh(scale * values * (1.0 + cubic * square))
    half = 0.5 * (1.0 + bend)
    slope = half + 0.5 * values * (1.0 - bend * bend) * scale * (1.0 + 3.0 * cubic * square)
    return values * half, slope


ROW_BLOCK = 256


def expert_kernel(
    slots, grad_out, w_in, w_out, small, here, result, activated, grad_part, grad_pre, grad_rows
):
    experts = here.shape[1]
    router = small[2 : 2 + experts, :].astype(BF16)
    probs = jax.nn.softmax(mm_nt(slots[...], router), axis=-1)
    gate = jnp.sum(probs * here[...], axis=-1, keepdims=True)
    low, slope = gelu_parts(mm(slots[...], w_in[...]))
    activated[...] = low.astype(BF16)
    grad_part[...] = (gate * grad_out[...].astype(F32)).astype(BF16)
    grad_pre[...] = (mm_nt(grad_part[...], w_out[...]) * slope).astype(BF16)
    result[...] = mm(activated[...], w_out[...]).astype(BF16)
    grad_gate = jnp.sum(
        grad_out[...].astype(F32) * result[...].astype(F32), axis=-1, keepdims=True
    )
    grad_logits = gate * grad_gate * (here[...] - probs)
    through_router = mm(grad_logits.astype(BF16), router)
    grad_rows[...] = (mm_nt(grad_pre[...], w_in[...]) + through_router).astype(BF16)


def expert_both(slots, grad_out, w_in, w_out, small, expert_count):
    expert = (lax.axis_index("z") * lax.axis_size("q") + lax.axis_index("q")) * 2 + lax.axis_index("h")
    here = (jnp.arange(expert_count, dtype=jnp.int32) == expert).astype(F32)[None]
    rows = slots.reshape(-1, slots.shape[-1])
    count, width = rows.shape
    hidden = w_in.shape[1]
    block = ROW_BLOCK if count % ROW_BLOCK == 0 else count

    def rows_of(size):
        return pl.BlockSpec((block, size), lambda step: (step, 0))

    def whole_of(array):
        return pl.BlockSpec(array.shape, lambda step: (0, 0))

    sizes = (width, hidden, width, hidden, width)
    result, activated, grad_part, grad_pre, grad_rows = pl.pallas_call(
        expert_kernel,
        grid=(count // block,),
        in_specs=[rows_of(width), rows_of(width)] + [whole_of(a) for a in (w_in, w_out, small, here)],
        out_specs=tuple(rows_of(size) for size in sizes),
        out_shape=tuple(jax.ShapeDtypeStruct((count, size), BF16) for size in sizes),
        compiler_params=pltpu.CompilerParams(vmem_limit_bytes=VMEM_BYTES),
        cost_estimate=pl.CostEstimate(
            flops=8 * count * width * hidden, bytes_accessed=16 * count * width, transcendentals=count * hidden
        ),
    )(rows, grad_out.reshape(rows.shape), w_in, w_out, small, here)
    kept = (rows, grad_pre, activated, grad_part)
    return kept, result.reshape(slots.shape), grad_rows.reshape(slots.shape)


def weight_grads_kernel(rows, grad_rows, grad_qkv, attended, grads):
    grads[...] = jnp.concatenate(
        [mm_tn(rows[...], grad_qkv[...]), mm_tn(grad_rows[...], attended[...])], axis=1
    ).astype(BF16)


def weight_grads(rows, grad_rows, grad_qkv, attended):
    width = grad_qkv.shape[1] + attended.shape[1]
    return whole_call(
        weight_grads_kernel,
        jax.ShapeDtypeStruct((rows.shape[1], width), BF16),
        rows,
        grad_rows,
        grad_qkv,
        attended,
        flops=2 * rows.size * width,
    )


def attention_forward(inputs, gathered, whole, group):
    values_in = inputs.astype(F32)
    rows_a, queries, keys_values, small = project(gathered, whole, group)
    own, other = gather_parts(keys_values)
    part, attended, attended_flat, log_total = attend(queries, own, other, whole)
    hidden = values_in + sum_chips(part)
    kept = (values_in, rows_a, queries, own, other, attended, attended_flat, log_total)
    return hidden, small, kept


def attention_backward(grad_hidden, small, kept, whole, last):
    values_in, rows_a, queries, own, other, attended, attended_flat, log_total = kept
    grad_rows = lax.all_gather(grad_hidden.astype(BF16), CHIPS, axis=0, tiled=True)
    grad_queries, grad_own, grad_other = attend_back(
        grad_rows, whole, queries, own, other, attended_flat, log_total
    )
    grad_qkv, part = project_back(grad_queries, sum_parts(grad_own, grad_other), whole)
    grads = weight_grads(rows_a, grad_rows, grad_qkv, attended)
    grad_normed_a = sum_chips(after(part, grads) if last else part)
    sums = scatter_now(grads) if last and lax.axis_size("q") == 1 else scatter_later(grads)
    inverse = lax.rsqrt(jnp.mean(values_in * values_in, axis=-1, keepdims=True) + EPSILON)
    grad_input_norm, grad_gain = norm_back(values_in, inverse, small[0:1], grad_normed_a)
    return (grad_hidden + grad_input_norm).astype(BF16), grad_gain, sums


def route_tokens(hidden, routes, small, expert_count):
    inverse_b, normed_b = norm_rows(hidden, small[1:2])
    router = small[2 : 2 + expert_count].astype(BF16)
    router_probs = jax.nn.softmax(mm_nt(normed_b, router), axis=-1)
    chosen = (
        routes.reshape(-1, 1) == jnp.arange(expert_count, dtype=jnp.int32)[None]
    ).astype(F32)
    gate = jnp.sum(router_probs * chosen, axis=-1, keepdims=True)
    return inverse_b, normed_b, router_probs, chosen, gate


def pack_rows(table, rows):
    wide = lax.axis_size("z") * lax.axis_size("q") * lax.axis_size("h")
    return mm(table, rows).astype(BF16).reshape(wide, -1, rows.shape[-1])


def unpack_rows(table, returned):
    return mm_tn(table, returned.reshape(table.shape[0], -1))


def expert_trip(slots, w_in, w_out):
    rows = slots.reshape(-1, slots.shape[-1])
    pre_act = mm(rows, w_in)
    activated = jax.nn.gelu(pre_act).astype(BF16)
    result = mm(activated, w_out).astype(BF16)
    return (rows, pre_act, activated), result.reshape(slots.shape)


def expert_trip_back(grad_slots, kept, w_in, w_out, extra=None):
    rows, pre_act, activated = kept
    grad_part = grad_slots.reshape(rows.shape)
    grad_act = mm_nt(grad_part, w_out)
    unused_value, gelu_back = jax.vjp(jax.nn.gelu, pre_act)
    grad_pre = gelu_back(grad_act)[0].astype(BF16)
    grad_rows = mm_nt(grad_pre, w_in)
    if extra is not None:
        grad_rows = grad_rows + extra
    return (rows, grad_pre, activated, grad_part), grad_rows.astype(BF16).reshape(grad_slots.shape)


def router_grads(grad_output, mixed, routed):
    inverse_b, normed_b, router_probs, chosen, gate = routed
    grad_gate = jnp.sum(grad_output * mixed, axis=-1, keepdims=True)
    grad_logits = gate * grad_gate * (chosen - router_probs)
    return grad_logits, dot(grad_logits, normed_b.astype(F32), ((0,), (0,)), HIGHEST)


def moe_norm_back(grad_output, grad_normed_b, hidden, routed, small):
    grad_hidden_norm, grad_gain = norm_back(hidden, routed[0], small[1:2], grad_normed_b)
    return grad_output + grad_hidden_norm, grad_gain


def shards(
    block_input,
    out_cotangent,
    routes,
    attn_gain,
    query_weight,
    key_weight,
    value_weight,
    output_weight,
    moe_gain,
    router_weight,
    expert_in,
    expert_out,
):
    micro_count, seq_count, half_rows, feature_dim = block_input.shape
    sequences = micro_count * seq_count
    expert_count = router_weight.shape[-1]
    most_rows = max(2, 3 * half_rows // (2 * expert_count))
    pipe, core = (lax.axis_index("pipe"), lax.axis_index("tp"))
    extra = -(-(2 + expert_count) // 128) * 128

    own_routes = lax.dynamic_slice_in_dim(
        routes[0, :, :, :, 0].reshape(sequences, -1), core * half_rows, half_rows, 1
    ).astype(BF16)
    other_routes = swapped(own_routes, "pipe")
    route_rows = jnp.stack(
        [
            jnp.where(pipe == 0, own_routes, other_routes),
            jnp.where(pipe == 0, other_routes, own_routes),
        ],
        axis=1,
    )
    route_rows = jnp.pad(route_rows, ((0, 0), (0, 14), (0, feature_dim - half_rows)))

    input_rows = jnp.concatenate(
        [
            block_input.reshape(sequences, half_rows, feature_dim),
            out_cotangent.reshape(sequences, half_rows, feature_dim),
            route_rows,
        ],
        axis=1,
    )
    here = to_planes(input_rows)
    cotangent = here[:, half_rows : 2 * half_rows].reshape(-1, feature_dim)
    inputs = here[:, :half_rows].reshape(-1, feature_dim)
    section_routes = [
        here[:, 2 * half_rows + section, :half_rows].astype(jnp.int32) for section in range(2)
    ]

    small = jnp.concatenate([attn_gain[0][:, None], moe_gain[0][:, None], router_weight[0]], axis=-1)
    small = jnp.pad(small, ((0, 0), (0, extra - small.shape[-1])))
    spread, gathered = spread_weights(
        query_weight[0], key_weight[0], value_weight[0], output_weight[0], small, inputs
    )
    group = query_weight.shape[-1] // 2

    first_whole = join_section(from_z(spread[:, 0]))
    whole = [first_whole, gather_later(after(spread[:, 1], first_whole))]
    w_in, w_out = (expert_in[0, 0], expert_out[0, 0])

    tables = [dispatch_table(rows, expert_count, most_rows) for rows in section_routes]
    hidden, first_small, kept_attn = attention_forward(inputs, gathered, whole[0], group)
    routed = route_tokens(hidden, section_routes[0], first_small, expert_count)
    packed, whole[1] = lax.optimization_barrier((pack_rows(tables[0], routed[1]), whole[1]))
    slots = to_experts((packed, pack_rows(tables[1], cotangent)))
    cotangent_slots = slots
    kept_expert, result = expert_trip(slots, w_in, w_out)
    mixed = unpack_rows(tables[0], from_experts(result, (0,)))
    first_output = (hidden + routed[4] * mixed).astype(BF16)
    first = (hidden, first_small, kept_attn, routed, kept_expert, mixed)

    gathered = lax.all_gather(first_output, CHIPS, axis=0, tiled=True)
    hidden, small, kept_attn = attention_forward(first_output, gathered, whole[1], group)
    routed = route_tokens(hidden, section_routes[1], small, expert_count)
    slots = to_experts((None, pack_rows(tables[1], routed[1])))
    part, second_result, grad_results = expert_both(
        slots, cotangent_slots, w_in, w_out, small, expert_count
    )
    expert_parts = [None, part]
    returned_grad = from_experts(grad_results, (1,))
    grad_output = cotangent.astype(F32)

    def by_pipe(first, second):
        return jnp.where(pipe == 0, first, second), jnp.where(pipe == 0, second, first)

    def paired(kept, got):
        return jnp.stack(by_pipe(kept, got), axis=1).reshape(sequences, -1, feature_dim)

    def to_owners(outputs, grads, small, sums):
        kept, sent = by_pipe(*grads)
        kept_small, sent_small = by_pipe(*small)
        count = kept_small.shape[0]
        got = swapped(jnp.concatenate([sent, sent_small.astype(BF16)], axis=0), "pipe")
        kept_small = kept_small + got[-count:].astype(F32)
        shape = (sequences // 2, half_rows, feature_dim)
        planes = lax.axis_size("z")
        by_plane = kept_small.astype(BF16).reshape(count, planes, -1).transpose(1, 0, 2)
        by_plane = jnp.pad(by_plane, ((0, 0), (0, 0), (0, feature_dim - by_plane.shape[-1])))
        both = jnp.concatenate(
            [outputs, paired(kept.reshape(shape), got[:-count].reshape(shape)), by_plane], axis=1
        )
        both, *sums = lax.optimization_barrier((both, *sums))
        chips = scatter_chips(sums)
        moved = exchanged_z(both)
        total = jnp.sum(moved[:, -count:, : feature_dim // planes].astype(F32), axis=0)
        rest = lax.axis_size("q") * lax.axis_size("h") * lax.axis_size("tp")
        by_rest = total.astype(BF16).reshape(count, rest, -1).transpose(1, 0, 2)
        small = jnp.sum(exchanged(after(by_rest, chips), ("q", "h", "tp")).astype(F32), axis=0)
        return moved, small, chips

    def small_rows(grad_gain_attn, grad_gain_moe, grad_router):
        stacked = jnp.concatenate([grad_gain_attn[None], grad_gain_moe[None], grad_router], axis=0)
        return jnp.pad(stacked, ((0, -stacked.shape[0] % 16), (0, 0)))

    grad_hidden, grad_gain_moe = moe_norm_back(
        grad_output, unpack_rows(tables[1], returned_grad), hidden, routed, small
    )
    second_grad, grad_gain_attn, sums_second = attention_backward(
        grad_hidden, small, kept_attn, whole[1], False
    )
    second = (hidden, routed, grad_output, grad_gain_attn, grad_gain_moe)

    hidden, small, kept_attn, routed, kept_expert, mixed = first
    grad_output = second_grad.astype(F32)
    grad_slots = to_experts((pack_rows(tables[0], (routed[4] * grad_output).astype(BF16)), None))
    expert_parts[0], grad_results = expert_trip_back(grad_slots, kept_expert, w_in, w_out)
    grad_logits, grad_router = router_grads(grad_output, mixed, routed)
    router = small[2 : 2 + expert_count].astype(BF16)
    grad_normed_router = mm(grad_logits.astype(BF16), router)
    slots, grad_pre, activated, grad_part = (
        jnp.where(pipe == 0, low, high) for low, high in zip(*expert_parts)
    )
    grad_w_in = mm_tn(slots, grad_pre)
    grad_w_out = mm_tn(activated, grad_part)
    returned = from_experts(jnp.where(pipe == 0, grad_results, second_result), (0, 1))
    count = returned.shape[1] // 2
    grad_hidden, grad_gain_moe = moe_norm_back(
        grad_output,
        grad_normed_router + unpack_rows(tables[0], returned[:, :count]),
        hidden,
        routed,
        small,
    )
    hidden, routed, grad_output, *gains = second
    mixed = unpack_rows(tables[1], returned[:, count:])
    second_output = (hidden + routed[4] * mixed).astype(BF16)
    small_second = small_rows(*gains, router_grads(grad_output, mixed, routed)[1])
    shape = (sequences // 2, half_rows, feature_dim)
    kept_output, sent_output = by_pipe(first_output, second_output)
    outputs = paired(kept_output.reshape(shape), swapped(sent_output, "pipe").reshape(shape))
    grad_hidden, grad_w_in, grad_w_out = lax.optimization_barrier(
        (grad_hidden, grad_w_in, grad_w_out)
    )
    first_grad, grad_gain_attn, sums_first = attention_backward(
        grad_hidden, small, kept_attn, whole[0], True
    )
    small_first = small_rows(grad_gain_attn, grad_gain_moe, grad_router)
    home, small, by_chip = to_owners(
        outputs,
        (first_grad, second_grad),
        (small_first, small_second),
        (sums_first, sums_second),
    )
    layer_outputs, grads_home = (
        home[:, begin : begin + half_rows].reshape(1, micro_count, seq_count, half_rows, feature_dim)
        for begin in (0, half_rows)
    )
    mats = scatter_end(by_chip)
    return (
        layer_outputs,
        grads_home,
        small[0][None],
        mats[0][None],
        mats[1][None],
        mats[2][None],
        mats[3].T[None],
        small[1][None],
        small[2 : 2 + expert_count].T[None],
        grad_w_in[None, None],
        grad_w_out[None, None],
    )


def solution(mesh):
    pipe, wide, tp = (mesh.shape["pipe"], mesh.shape["wide"], mesh.shape["tp"])
    planes = Mesh(mesh.devices.reshape(pipe, 4, wide // 8, 2, tp), ("pipe", "z", "q", "h", "tp"))
    rows = WIDE + ("tp",)
    placed = (
        P(None, None, rows, None),
        P(None, None, rows, None),
        P("pipe", None, None, WIDE, None),
        P("pipe", rows),
        P("pipe", WIDE, "tp"),
        P("pipe", WIDE, "tp"),
        P("pipe", WIDE, "tp"),
        P("pipe", "tp", WIDE),
        P("pipe", rows),
        P("pipe", rows, None),
        P("pipe", WIDE, None, "tp"),
        P("pipe", WIDE, "tp", None),
    )
    return jax.shard_map(
        shards,
        mesh=planes,
        in_specs=placed,
        out_specs=(
            P("pipe", None, None, rows, None),
            P("pipe", None, None, rows, None),
            P("pipe", rows),
            P("pipe", WIDE, "tp"),
            P("pipe", WIDE, "tp"),
            P("pipe", WIDE, "tp"),
            P("pipe", "tp", WIDE),
            P("pipe", rows),
            P("pipe", rows, None),
            P("pipe", WIDE, None, "tp"),
            P("pipe", WIDE, "tp", None),
        ),
        check_vma=False,
    )
```
